32 devices in a mesh: dp: 2 (over x), seq: 16 (over z, y, core).
Axes of the slice: x: 2, y: 2, z: 4, core: 2. Of those that a mesh axis runs over, the one named last changes fastest.
Arguments:
- queries: bfloat16 [2, 16, 512, 1024], P('dp', 'seq'), may hold values from -16 to 16
- keys: bfloat16 [2, 16, 512, 1024], P('dp', 'seq'), may hold values from -12 to 12
- values: bfloat16 [2, 16, 512, 1024], P('dp', 'seq'), may hold values from -24 to 24
- out_proj: bfloat16 [1024, 2048], P(('dp', 'seq')), may hold values from -0.1875 to 0.1875
- out_grad: bfloat16 [2, 16, 512, 2048], P('dp', 'seq'), may hold values from -48 to 48
- block_pattern: int32 [4, 4], replicated, may hold values from 0 to 3, as said below
- col_offset: int32 [4], replicated, may hold values from 0 to 511
Outputs:
- layer_out: bfloat16 [2, 16, 512, 2048], P('dp', 'seq')
- q_grad: bfloat16 [2, 16, 512, 1024], P('dp', 'seq')
- k_grad: bfloat16 [2, 16, 512, 1024], P('dp', 'seq')
- v_grad: bfloat16 [2, 16, 512, 1024], P('dp', 'seq')
- w_grad: float32 [1024, 2048], P(('dp', 'seq'))
The draws below stay inside these ranges and needn't reach their ends.
Inputs may be any that keep to these rules, and one draw needn't show every extreme that they name: `block_pattern`: for each row head, the entries name each of the 4 blocks of a grid row once, and entry j is never j.
All inputs are finite; a program needn't handle non-finite values.
Results may differ from the reference program's by a relative error of at most 0.006.
Values may be sent and summed in bfloat16 or wider, within the bound.
A program may use at most 128 MiB of HBM per device.

```python
import jax
import jax.numpy as jnp
from jax import lax

D = 2048
HD = 128
HR = 4
HC = 4
BLK = 128
NB = 4
W = 1024
COLS = 512
GR = 16
BATCH = 2
ALL_TOK = 16384


def draw_queries(key, part):
    full_shape = (BATCH, GR, COLS, W)
    base_key = jax.random.fold_in(key, 101)
    result_field = jnp.clip(jax.random.normal(jax.random.fold_in(base_key, 1), full_shape, jnp.float32), -6.0, 6.0)
    return result_field.astype(jnp.bfloat16)


def draw_keys(key, part):
    full_shape = (BATCH, GR, COLS, W)
    base_key = jax.random.fold_in(key, 202)
    result_field = jnp.clip(jax.random.normal(jax.random.fold_in(base_key, 1), full_shape, jnp.float32), -6.0, 6.0)
    return result_field.astype(jnp.bfloat16)


def draw_block_pattern(key, part):
    head_keys = jax.random.split(jax.random.fold_in(key, 303), HR)

    def one_head(head_key):
        block_order = jax.random.permutation(head_key, NB).astype(jnp.int32)
        next_block = jnp.roll(block_order, -1)
        return jnp.zeros((NB,), jnp.int32).at[block_order].set(next_block)
    return jax.vmap(one_head)(head_keys).astype(jnp.int32)


def place_ends(result, key, least, largest):
    longest = result.shape.index(max(result.shape))
    spots = []
    for shift in (0, 1):
        where = [jax.random.randint(jax.random.fold_in(key, axis), (), 0, length) for axis, length in enumerate(result.shape)]
        where[longest] = (where[longest] + shift) % result.shape[longest]
        spots.append(tuple(where))
    return result.at[spots[0]].set(least).at[spots[1]].set(largest)


def strengthened(values, own_key, source, target, blocks, factor):
    owner, partner = [(jnp.arange(values.shape[axis_at]) // (values.shape[axis_at] // blocks)).reshape([-1 if axis == axis_at else 1 for axis in range(values.ndim)]) for axis_at in (source, target)]
    chosen = jax.random.permutation(own_key, blocks)[partner]
    strong = (owner == chosen) | (owner == (partner + blocks // 2) % blocks)
    return jnp.where(strong, factor * values, values)


def block_scale(key, shape, cuts, low, largest):
    factor_of, own = 1.0, jax.random.fold_in(key, 6)
    for position, shards_of in cuts:
        draws = jnp.exp(jax.random.uniform(jax.random.fold_in(own, position), (shards_of,), jnp.float32, low / len(cuts), largest / len(cuts)))
        factor_of = factor_of * jnp.repeat(draws, shape[position] // shards_of).reshape([-1 if axis == position else 1 for axis in range(len(shape))])
    return factor_of


def normal_values(rng, dims, deviation, bound, cuts=(), kind=jnp.bfloat16):
    array = jax.random.normal(rng, dims, jnp.float32) * deviation
    if len(cuts) > 0:
        array = block_scale(rng, dims, cuts, -0.22, 0.18) * array
    return jnp.clip(array, min=-bound, max=bound).astype(kind)


def noise_with(own_key, dims, scale, bound, cuts, heavy, kind=jnp.bfloat16):
    drawn = scale * jax.random.normal(own_key, dims, jnp.float32)
    if cuts:
        drawn = drawn * block_scale(own_key, dims, cuts, -0.22, 0.18)
    return jnp.clip(strengthened(drawn, jax.random.fold_in(own_key, 3), *heavy), -bound, bound).astype(kind)


def setup_inputs(seed: int = 0) -> dict:
    seeds = jax.random.split(jax.random.key(seed), 8)
    return {
        "queries": draw_queries(jax.random.fold_in(seeds[7], 71), 0),
        "keys": draw_keys(jax.random.fold_in(seeds[7], 71), 0),
        "values": normal_values(seeds[2], (BATCH, GR, COLS, W), 4.0, 24.0, ((0, 2), (1, 16))),
        "out_proj": normal_values(seeds[3], (W, D), W ** -0.5, 0.1875, ((0, 32),)),
        "out_grad": noise_with(seeds[4], (BATCH, GR, COLS, D), 8.0, 48.0, ((0, 2), (1, 16)), (1, 3, 16, 2.0)),
        "block_pattern": draw_block_pattern(jax.random.fold_in(seeds[7], 71), 0),
        "col_offset": place_ends(jax.random.randint(seeds[6], (HC,), 0, COLS), jax.random.fold_in(seeds[6], 1), 0, COLS - 1).astype(jnp.int32),
    }


def half_and_back(tensor):
    return lax.optimization_barrier(tensor.astype(jnp.bfloat16)).astype(jnp.float32)


def row_head(query_h, key_h, value_h, grad_h, pattern_h):
    score_scale = HD ** -0.5
    query_full = query_h.astype(jnp.float32)
    grad_full = grad_h.astype(jnp.float32)
    key_joined = jnp.concatenate([jnp.take(key_h, pattern_h, axis=1), key_h], axis=2).astype(jnp.float32)
    value_joined = jnp.concatenate([jnp.take(value_h, pattern_h, axis=1), value_h], axis=2).astype(jnp.float32)
    scores = jnp.einsum('rjqd,rjkd->rjqk', query_full, key_joined) * score_scale
    row_probs = jax.nn.softmax(scores, axis=-1)
    prob_half = half_and_back(row_probs)
    head_out = jnp.einsum('rjqk,rjkd->rjqd', prob_half, value_joined).astype(jnp.bfloat16)
    value_terms = jnp.einsum('rjqk,rjqd->rjkd', prob_half, grad_full)
    prob_grad = jnp.einsum('rjqd,rjkd->rjqk', grad_full, value_joined)
    delta_sum = jnp.sum(row_probs * prob_grad, axis=-1, keepdims=True)
    score_grad = half_and_back(row_probs * (prob_grad - delta_sum))
    query_grad = (jnp.einsum('rjqk,rjkd->rjqd', score_grad, key_joined) * score_scale).astype(jnp.bfloat16)
    key_terms = jnp.einsum('rjqk,rjqd->rjkd', score_grad, query_full) * score_scale
    key_grad = key_terms[:, :, BLK:].at[:, pattern_h].add(key_terms[:, :, :BLK]).astype(jnp.bfloat16)
    value_grad = value_terms[:, :, BLK:].at[:, pattern_h].add(value_terms[:, :, :BLK]).astype(jnp.bfloat16)
    return head_out, query_grad, key_grad, value_grad


def column_head(query_h, key_h, value_h, grad_h, offset_h):
    score_scale = HD ** -0.5
    query_full = query_h.astype(jnp.float32)
    grad_full = grad_h.astype(jnp.float32)
    key_moved = jnp.roll(key_h, offset_h, axis=1).astype(jnp.float32)
    value_moved = jnp.roll(value_h, offset_h, axis=1).astype(jnp.float32)
    scores = jnp.einsum('rcd,scd->crs', query_full, key_moved) * score_scale
    col_probs = jax.nn.softmax(scores, axis=-1)
    prob_half = half_and_back(col_probs)
    head_out = jnp.einsum('crs,scd->rcd', prob_half, value_moved).astype(jnp.bfloat16)
    value_terms = jnp.einsum('crs,rcd->scd', prob_half, grad_full)
    prob_grad = jnp.einsum('rcd,scd->crs', grad_full, value_moved)
    delta_sum = jnp.sum(col_probs * prob_grad, axis=-1, keepdims=True)
    score_grad = half_and_back(col_probs * (prob_grad - delta_sum))
    query_grad = (jnp.einsum('crs,scd->rcd', score_grad, key_moved) * score_scale).astype(jnp.bfloat16)
    key_terms = jnp.einsum('crs,rcd->scd', score_grad, query_full) * score_scale
    key_grad = jnp.roll(key_terms, -offset_h, axis=1).astype(jnp.bfloat16)
    value_grad = jnp.roll(value_terms, -offset_h, axis=1).astype(jnp.bfloat16)
    return head_out, query_grad, key_grad, value_grad


def one_sequence(query_seq, key_seq, value_seq, grad_seq, out_proj, block_pattern, col_offset):
    head_count = HR + HC
    grad_flat = grad_seq.reshape(GR * COLS, D)
    attn_grad = jnp.dot(grad_flat, out_proj.T, preferred_element_type=jnp.float32).astype(jnp.bfloat16)
    grad_heads = attn_grad.reshape(GR, COLS, head_count, HD)
    query_heads = query_seq.reshape(GR, COLS, head_count, HD)
    key_heads = key_seq.reshape(GR, COLS, head_count, HD)
    value_heads = value_seq.reshape(GR, COLS, head_count, HD)
    collected = ([], [], [], [])
    block_shape = (GR, NB, BLK, HD)
    for head_idx in range(HR):
        results = row_head(query_heads[:, :, head_idx].reshape(block_shape),
                           key_heads[:, :, head_idx].reshape(block_shape),
                           value_heads[:, :, head_idx].reshape(block_shape),
                           grad_heads[:, :, head_idx].reshape(block_shape),
                           block_pattern[head_idx])
        for target, result_part in zip(collected, results):
            target.append(result_part.reshape(GR, COLS, HD))
    for col_idx in range(HC):
        head_idx = HR + col_idx
        results = column_head(query_heads[:, :, head_idx], key_heads[:, :, head_idx],
                              value_heads[:, :, head_idx], grad_heads[:, :, head_idx],
                              col_offset[col_idx])
        for target, result_part in zip(collected, results):
            target.append(result_part)

    def merge_heads(pieces):
        return jnp.stack(pieces, axis=2).reshape(GR, COLS, head_count * HD)

    attention = merge_heads(collected[0])
    attn_flat = attention.reshape(GR * COLS, head_count * HD)
    layer_out = jnp.dot(attn_flat, out_proj, preferred_element_type=jnp.float32).astype(jnp.bfloat16).reshape(GR, COLS, D)
    grad_part = jnp.dot(attn_flat.T, grad_flat, preferred_element_type=jnp.float32)
    return layer_out, merge_heads(collected[1]), merge_heads(collected[2]), merge_heads(collected[3]), grad_part


def reference(queries, keys, values, out_proj, out_grad, block_pattern, col_offset):
    def per_sequence(inputs):
        return one_sequence(inputs[0], inputs[1], inputs[2], inputs[3], out_proj, block_pattern, col_offset)

    layer_out, q_grad, k_grad, v_grad, grad_parts = lax.map(per_sequence, (queries, keys, values, out_grad))
    w_grad = jnp.sum(grad_parts, axis=0) * (ALL_TOK ** -0.5)
    return layer_out, q_grad, k_grad, v_grad, w_grad
```

```python
import functools

import jax
import jax.numpy as jnp
from jax import lax
from jax.experimental import pallas as pl
from jax.experimental.pallas import tpu as pltpu
from jax.sharding import PartitionSpec as P

HD = 128
HR = 4
HC = 4
BLK = 128
NB = 4
HALF = HR * HD
CHUNKS = 4
SCALE = HD ** (-0.5)
NEG = -1e30
MESH = pl.DeviceIdType.MESH
F32 = jnp.float32
BF16 = jnp.bfloat16


def nt(a, b):
    return lax.dot_general(a, b, (((1,), (1,)), ((), ())), preferred_element_type=F32)


def nn(a, b):
    return jnp.dot(a, b, preferred_element_type=F32)


def tn(a, b):
    return lax.dot_general(a, b, (((0,), (0,)), ((), ())), preferred_element_type=F32)


def probs(query, key, bias):
    scores = nt(query, key) * SCALE + bias
    shifted = jnp.exp(scores - jnp.max(scores, axis=-1, keepdims=True))
    return shifted * (1.0 / jnp.sum(shifted, axis=-1, keepdims=True))


def score_grads(prob, grad, value):
    prob_grad = nt(grad, value)
    delta_sum = jnp.sum(prob * prob_grad, axis=-1, keepdims=True)
    return (prob * (prob_grad - delta_sum)).astype(BF16)


def head_cols(head_idx):
    return pl.ds(pl.multiple_of(head_idx * HD, HD), HD)


def body(seq, inside, q, k, v, w_in, og, pattern, offset, lo, dq, dk, dv, wg,
         w_all, grads, att, att_t, col_in, col_src, col_bias, col_prob, p_scr, s_scr,
         wp, core_in, keep, x_src, x_in, z_src, z_in,
         a_send, a_recv, g_send, g_recv, c_send, c_recv, x_send, x_recv, z_send, z_recv):
    tokens = q.shape[0]
    cols = tokens // seq
    width = og.shape[1]
    piece = width // CHUNKS
    pairs = seq // 2
    me = lax.axis_index("seq")
    dp = lax.axis_index("dp")
    core = lax.rem(me, 2)
    pair = me // 2
    y_at = lax.rem(pair, 2)
    z_at = pair // 2
    depth = seq // 4

    barrier = pltpu.get_barrier_semaphore()

    def greet(step, carry):
        pl.semaphore_signal(
            barrier, inc=1, device_id=(dp, lax.rem(me + step, seq)), device_id_type=MESH
        )
        return carry

    lax.fori_loop(1, seq, greet, 0)
    if inside:
        pl.semaphore_signal(barrier, inc=1, device_id=(1 - dp, me), device_id_type=MESH)
    pl.semaphore_wait(barrier, seq if inside else seq - 1)

    def push(src, dst, send, recv, target):
        pltpu.make_async_remote_copy(
            src_ref=src, dst_ref=dst, send_sem=send, recv_sem=recv,
            device_id=target, device_id_type=MESH,
        ).start()

    def drain(ref, sem):
        pltpu.make_async_copy(ref, ref, sem).wait()

    def col_rows(peer):
        return pl.ds(pl.multiple_of(peer * cols, cols), cols)

    def spread(source, slot):
        def one(step, carry):
            peer = lax.rem(me + step, seq)
            push(source(peer), col_in.at[slot, me], a_send.at[slot], a_recv.at[slot], (dp, peer))
            return carry

        lax.fori_loop(1, seq, one, 0)

    def arrived(slot):
        drain(col_in.at[slot, pl.ds(0, seq - 1)], a_recv.at[slot])

    def piece_cols(c):
        return pl.ds(pl.multiple_of(c * piece, piece), piece)

    if inside:
        w_all[dp, z_at, y_at, core] = w_in[...]
        for c in range(CHUNKS):
            def z_step(step, carry, c=c):
                z_to = lax.rem(z_at + step, depth)
                block = w_all.at[dp, z_at, y_at, core, :, piece_cols(c)]
                push(block, block, g_send.at[0, c], g_recv.at[0, c],
                     (dp, (z_to * 2 + y_at) * 2 + core))
                return carry

            lax.fori_loop(1, depth, z_step, 0)
        weights = w_all
    else:
        weights = w_in

    spread(lambda peer: q.at[col_rows(peer), pl.ds(HALF, HALF)], 0)
    col_in[0, me] = q[col_rows(me), HALF:]

    row_at = lax.broadcasted_iota(jnp.int32, (tokens, tokens), 0)
    lane_at = lax.broadcasted_iota(jnp.int32, (tokens, tokens), 1)

    def moved(tensor, head_idx, forth):
        apart = (row_at - lane_at if forth else lane_at - row_at) - offset[head_idx]
        chosen = jnp.where((apart == 0) | (apart == -tokens), 1.0, 0.0).astype(BF16)
        return nn(chosen, tensor).astype(BF16)

    for tensor, src_slot, slot in ((k, 0, 1), (v, 1, 2)):
        for head_idx in range(HC):
            shifted = moved(tensor[:, HALF + head_idx * HD:HALF + (head_idx + 1) * HD], head_idx, True)
            col_src[src_slot, :, :, head_idx * HD:(head_idx + 1) * HD] = shifted.reshape(seq, cols, HD)
        spread(lambda peer, s=src_slot: col_src.at[s, peer], slot)
        col_in[slot, me] = col_src[src_slot, me]

    part_row = lax.broadcasted_iota(jnp.int32, (BLK, tokens), 0)
    part_lane = lax.broadcasted_iota(jnp.int32, (BLK, tokens), 1)
    col_bias[...] = jnp.where(lax.rem(part_row, cols) == lax.rem(part_lane, cols), 0.0, NEG)

    if inside:
        for c in range(CHUNKS):
            drain(w_all.at[0, pl.ds(0, depth - 1), 0, 0, :, piece_cols(c)], g_recv.at[0, c])
            block = w_all.at[dp, :, y_at, core, :, piece_cols(c)]
            push(block, block, g_send.at[1, c], g_recv.at[1, c],
                 (dp, (z_at * 2 + 1 - y_at) * 2 + core))
        for c in range(CHUNKS):
            drain(w_all.at[0, :, 0, 0, :, piece_cols(c)], g_recv.at[1, c])
            block = w_all.at[dp, :, :, core, :, piece_cols(c)]
            push(block, block, g_send.at[2, c], g_recv.at[2, c], (1 - dp, me))
        for c in range(CHUNKS):
            drain(w_all.at[0, :, :, 0, :, piece_cols(c)], g_recv.at[2, c])
            block = w_all.at[:, :, :, core, :, piece_cols(c)]
            push(block, block, g_send.at[3, c], g_recv.at[3, c], (dp, pair * 2 + 1 - core))
        for c in range(CHUNKS):
            drain(w_all.at[:, :, :, 0, :, piece_cols(c)], g_recv.at[3, c])

    tall = 256
    steps = tall // (4 * weights.shape[4])

    def attn_grad(half):
        def one(n, carry):
            rows = weights[half, pl.ds(n * steps, steps)].reshape(tall, width)
            part = nt(og[...], rows).astype(BF16)
            grads[:, pl.ds(pl.multiple_of(half * HALF + n * tall, tall), tall)] = part
            return carry

        lax.fori_loop(0, HALF // tall, one, 0)

    attn_grad(1)
    spread(lambda peer: grads.at[col_rows(peer), pl.ds(HALF, HALF)], 3)
    col_in[3, me] = grads[col_rows(me), HALF:]

    part_slots = BLK // cols

    def col_block(ref, slot, part, where):
        return ref[slot, part * part_slots:(part + 1) * part_slots, :, where].reshape(BLK, HD)

    def col_full(ref, slot, where):
        return ref[slot, :, :, where].reshape(tokens, HD)

    def col_put(slot, part, where, val):
        col_src[slot, part * part_slots:(part + 1) * part_slots, :, where] = (
            val.astype(BF16).reshape(part_slots, cols, HD))

    parts = tokens // BLK
    arrived(0)
    arrived(1)
    arrived(2)

    def col_forward(head_idx, carry):
        where = head_cols(head_idx)
        key, value = col_full(col_in, 1, where), col_full(col_in, 2, where)
        for part in range(parts):
            prob = probs(col_block(col_in, 0, part, where), key, col_bias[...])
            col_prob[head_idx, part * BLK:(part + 1) * BLK] = prob
            col_put(2, part, where, nn(prob.astype(BF16), value))
        return carry

    lax.fori_loop(0, HC, col_forward, 0)
    spread(lambda peer: col_src.at[2, peer], 4)
    col_in[4, me] = col_src[2, me]

    attn_grad(0)
    key_block = lax.broadcasted_iota(jnp.int32, (1, tokens), 1) // BLK

    def row_head(head_idx, carry):
        where = head_cols(head_idx)
        key, value = k[:, where], v[:, where]
        for part in range(parts):
            rows = slice(part * BLK, (part + 1) * BLK)
            seen = (key_block == part) | (key_block == pattern[head_idx, part])
            prob = probs(q[rows, where], key, jnp.where(seen, 0.0, NEG))
            half_prob = prob.astype(BF16)
            att[rows, where] = nn(half_prob, value).astype(BF16)
            score_grad = score_grads(prob, grads[rows, where], value)
            dq[rows, where] = (nn(score_grad, key) * SCALE).astype(BF16)
            p_scr[rows] = half_prob
            s_scr[rows] = score_grad
        dk[:, where] = (tn(s_scr[...], q[:, where]) * SCALE).astype(BF16)
        dv[:, where] = tn(p_scr[...], grads[:, where]).astype(BF16)
        return carry

    lax.fori_loop(0, HR, row_head, 0)

    def w_part(half):
        att_t[...] = att[:, half * HALF:(half + 1) * HALF].astype(F32).T.astype(BF16)

        def one(c, carry):
            at = piece_cols(c)
            product = nn(att_t[...], og[:, at])
            if inside:
                wp[half, :, :, :, at] = product.astype(BF16).reshape(pairs, 2, HALF // seq, piece)
                push(wp.at[half, :, 1 - core, :, at], core_in.at[half, :, :, at],
                     c_send.at[half, c], c_recv.at[half, c], (dp, pair * 2 + 1 - core))
            else:
                wg[pl.ds(half * HALF, HALF), at] = product
            return carry

        lax.fori_loop(0, CHUNKS, one, 0)

    w_part(0)

    arrived(3)

    def col_backward(head_idx, carry):
        where = head_cols(head_idx)
        key, value = col_full(col_in, 1, where), col_full(col_in, 2, where)
        for part in range(parts):
            rows = slice(part * BLK, (part + 1) * BLK)
            prob = col_prob[head_idx, rows]
            score_grad = score_grads(prob, col_block(col_in, 3, part, where), value)
            col_put(3, part, where, nn(score_grad, key) * SCALE)
            p_scr[rows] = prob.astype(BF16)
            s_scr[rows] = score_grad
        key_grad = tn(s_scr[...], col_full(col_in, 0, where)) * SCALE
        value_grad = tn(p_scr[...], col_full(col_in, 3, where))
        col_src[4, :, :, where] = key_grad.astype(BF16).reshape(seq, cols, HD)
        col_src[5, :, :, where] = value_grad.astype(BF16).reshape(seq, cols, HD)
        return carry

    lax.fori_loop(0, HC, col_backward, 0)

    arrived(4)
    att[:, HALF:] = col_in[4].reshape(tokens, HALF)
    w_part(1)
    for slot in (5, 6, 7):
        spread(lambda peer, s=slot - 2: col_src.at[s, peer], slot)
        col_in[slot, me] = col_src[slot - 2, me]

    if inside:
        def x_step(c, carry):
            at = piece_cols(c)
            for half in (0, 1):
                drain(core_in.at[half, :, :, at], c_recv.at[half, c])
            keep[:, :, at] = wp[dp, :, core, :, at].astype(F32) + core_in[dp, :, :, at].astype(F32)
            x_src[:, :, at] = (
                wp[1 - dp, :, core, :, at].astype(F32) + core_in[1 - dp, :, :, at].astype(F32)
            ).astype(BF16)
            push(x_src.at[:, :, at], x_in.at[:, :, at], x_send.at[c], x_recv.at[c], (1 - dp, me))
            return carry

        lax.fori_loop(0, CHUNKS, x_step, 0)

    def layer(n, carry):
        at = pl.ds(pl.multiple_of(n * tall, tall), tall)
        lo[:, at] = nn(att[...], weights[:, :, :, :, :, at].reshape(2 * HALF, tall)).astype(BF16)
        return carry

    lax.fori_loop(0, width // tall, layer, 0)

    if inside:
        def z_step(c, carry):
            at = piece_cols(c)
            drain(x_in.at[:, :, at], x_recv.at[c])
            z_src[:, :, at] = (keep[:, :, at] + x_in[:, :, at].astype(F32)).astype(BF16)
            z_in[pair, :, at] = z_src[pair, :, at]

            def one(step, inner):
                peer = lax.rem(pair + step, pairs)
                push(z_src.at[peer, :, at], z_in.at[pair, :, at], z_send.at[c], z_recv.at[c],
                     (dp, peer * 2 + core))
                return inner

            lax.fori_loop(1, pairs, one, 0)
            return carry

        lax.fori_loop(0, CHUNKS, z_step, 0)

    arrived(5)
    dq[:, HALF:] = col_in[5].reshape(tokens, HALF)
    for slot, target in ((6, dk), (7, dv)):
        arrived(slot)
        for head_idx in range(HC):
            lanes = slice(head_idx * HD, (head_idx + 1) * HD)
            back = moved(col_in[slot, :, :, lanes].reshape(tokens, HD), head_idx, False)
            target[:, HALF + head_idx * HD:HALF + (head_idx + 1) * HD] = back

    if inside:
        factor = (2 * seq * tokens) ** (-0.5)
        for c in range(CHUNKS):
            at = piece_cols(c)
            drain(z_in.at[pl.ds(0, pairs - 1), :, at], z_recv.at[c])
            wg[:, at] = jnp.sum(z_in[:, :, at].astype(F32), axis=0) * factor
        for c in range(CHUNKS):
            drain(w_all.at[0, pl.ds(0, depth - 1), 0, 0, :, piece_cols(c)], g_send.at[0, c])
            drain(w_all.at[0, :, 0, 0, :, piece_cols(c)], g_send.at[1, c])
            drain(w_all.at[0, :, :, 0, :, piece_cols(c)], g_send.at[2, c])
            drain(w_all.at[:, :, :, 0, :, piece_cols(c)], g_send.at[3, c])
            for half in (0, 1):
                drain(core_in.at[half, :, :, piece_cols(c)], c_send.at[half, c])
            drain(x_in.at[:, :, piece_cols(c)], x_send.at[c])
            drain(z_in.at[pl.ds(0, pairs - 1), :, piece_cols(c)], z_send.at[c])
    for slot in range(8):
        drain(col_in.at[slot, pl.ds(0, seq - 1)], a_send.at[slot])


def shards(dp_count, seq, queries, keys, values, out_proj, out_grad, block_pattern, col_offset):
    tokens, feats = queries.shape[2:]
    width = out_grad.shape[3]
    share = out_proj.shape[0]
    cols = tokens // seq
    inside = dp_count == 2 and share % 16 == 0
    split = (2, seq // 4, 2, 2, feats // (2 * seq), width)
    if inside:
        w_in = out_proj
    else:
        w_in = lax.all_gather(out_proj, ("dp", "seq"), axis=0, tiled=True).reshape(split)
    small = lambda shape, kind: pltpu.VMEM(shape if inside else (16, 128), kind)
    group = (seq // 2, share, width)
    sems = pltpu.SemaphoreType.DMA
    vmem = pl.BlockSpec(memory_space=pltpu.VMEM)
    smem = pl.BlockSpec(memory_space=pltpu.SMEM)
    flat = jax.ShapeDtypeStruct((tokens, feats), BF16)
    outs = pl.pallas_call(
        functools.partial(body, seq, inside),
        out_shape=[
            jax.ShapeDtypeStruct((tokens, width), BF16), flat, flat, flat,
            jax.ShapeDtypeStruct((share if inside else feats, width), F32),
        ],
        in_specs=[vmem] * 5 + [smem] * 2,
        out_specs=[vmem] * 5,
        scratch_shapes=[
            small(split, BF16),
            pltpu.VMEM((tokens, feats), BF16),
            pltpu.VMEM((tokens, feats), BF16),
            pltpu.VMEM((HALF, tokens), BF16),
            pltpu.VMEM((8, seq, cols, HALF), BF16),
            pltpu.VMEM((6, seq, cols, HALF), BF16),
            pltpu.VMEM((BLK, tokens), F32),
            pltpu.VMEM((HC, tokens, tokens), F32),
            pltpu.VMEM((tokens, tokens), BF16),
            pltpu.VMEM((tokens, tokens), BF16),
            small((2, seq // 2, 2, share, width), BF16),
            small((2,) + group, BF16),
            small(group, F32),
            small(group, BF16),
            small(group, BF16),
            small(group, BF16),
            small(group, BF16),
            sems((8,)), sems((8,)),
            sems((4, CHUNKS)), sems((4, CHUNKS)),
            sems((2, CHUNKS)), sems((2, CHUNKS)),
            sems((CHUNKS,)), sems((CHUNKS,)),
            sems((CHUNKS,)), sems((CHUNKS,)),
        ],
        compiler_params=pltpu.CompilerParams(
            collective_id=0, has_side_effects=True, vmem_limit_bytes=58 * 2 ** 20
        ),
        cost_estimate=pl.CostEstimate(
            flops=12 * 10 ** 9, bytes_accessed=11 * 2 ** 20, transcendentals=2 * 2 ** 20
        ),
    )(
        queries.reshape(tokens, feats), keys.reshape(tokens, feats), values.reshape(tokens, feats),
        w_in, out_grad.reshape(tokens, width), block_pattern, col_offset,
    )
    layer_out, q_grad, k_grad, v_grad, w_grad = outs
    if not inside:
        w_grad = lax.psum_scatter(w_grad, ("dp", "seq"), scatter_dimension=0, tiled=True)
        w_grad = w_grad * (dp_count * seq * tokens) ** (-0.5)
    shape = (1, 1, tokens, feats)
    return (
        layer_out.reshape(1, 1, tokens, width),
        q_grad.reshape(shape), k_grad.reshape(shape), v_grad.reshape(shape), w_grad,
    )


def solution(mesh):
    rows = P("dp", "seq", None, None)
    flat = P(("dp", "seq"), None)
    in_specs = (rows, rows, rows, flat, rows, P(), P())
    out_specs = (rows, rows, rows, rows, flat)
    return jax.shard_map(
        functools.partial(shards, mesh.shape["dp"], mesh.shape["seq"]),
        mesh=mesh, in_specs=in_specs, out_specs=out_specs, check_vma=False,
    )
```

```python
import functools

import jax
import jax.numpy as jnp
from jax import lax
from jax.experimental import pallas as pl
from jax.experimental.pallas import tpu as pltpu
from jax.sharding import PartitionSpec as P

HD = 128
HR = 4
HC = 4
BLK = 128
NB = 4
HALF = HR * HD
CHUNKS = 4
SCALE = HD ** (-0.5)
NEG = -1e30
MESH = pl.DeviceIdType.MESH
F32 = jnp.float32
BF16 = jnp.bfloat16


def nt(a, b):
    return lax.dot_general(a, b, (((1,), (1,)), ((), ())), preferred_element_type=F32)


def nn(a, b):
    return jnp.dot(a, b, preferred_element_type=F32)


def tn(a, b):
    return lax.dot_general(a, b, (((0,), (0,)), ((), ())), preferred_element_type=F32)


def probs(query, key, bias):
    scores = nt(query, key) * SCALE + bias
    shifted = jnp.exp(scores - jnp.max(scores, axis=-1, keepdims=True))
    return shifted * (1.0 / jnp.sum(shifted, axis=-1, keepdims=True))


def score_grads(prob, grad, value):
    prob_grad = nt(grad, value)
    delta_sum = jnp.sum(prob * prob_grad, axis=-1, keepdims=True)
    return (prob * (prob_grad - delta_sum)).astype(BF16)


def head_cols(head_idx):
    return pl.ds(pl.multiple_of(head_idx * HD, HD), HD)


def body(seq, inside, q_far, k_far, v_far, w_far, og_far, pattern, offset, lo, dq, dk, dv, wg,
         q, k, v, w_in, og, l_sem, w_all, grads, att, att_t, col_in, col_src, col_bias, col_prob, p_scr, s_scr,
         wp, core_in, y_src, y_in, keep, x_src, x_in, z_src, z_in,
         a_send, a_recv, g_send, g_recv, c_send, c_recv, y_send, y_recv, x_send, x_recv, z_send, z_recv):
    tokens = q.shape[0]
    cols = tokens // seq
    width = og.shape[1]
    piece = width // CHUNKS
    me = lax.axis_index("seq")
    dp = lax.axis_index("dp")
    core = lax.rem(me, 2)
    pair = me // 2
    y_at = lax.rem(pair, 2)
    z_at = pair // 2
    depth = seq // 4

    near = [pltpu.make_async_copy(far, close, l_sem.at[at]) for at, (far, close) in enumerate(
        ((w_far, w_in), (k_far, k), (q_far, q), (v_far, v), (og_far, og)))]
    for load in near:
        load.start()

    barrier = pltpu.get_barrier_semaphore()

    def greet(step, carry):
        pl.semaphore_signal(
            barrier, inc=1, device_id=(dp, lax.rem(me + step, seq)), device_id_type=MESH
        )
        return carry

    lax.fori_loop(1, seq, greet, 0)
    if inside:
        pl.semaphore_signal(barrier, inc=1, device_id=(1 - dp, me), device_id_type=MESH)
    pl.semaphore_wait(barrier, seq if inside else seq - 1)

    def push(src, dst, send, recv, target):
        pltpu.make_async_remote_copy(
            src_ref=src, dst_ref=dst, send_sem=send, recv_sem=recv,
            device_id=target, device_id_type=MESH,
        ).start()

    def drain(ref, sem):
        pltpu.make_async_copy(ref, ref, sem).wait()

    def col_rows(peer):
        return pl.ds(pl.multiple_of(peer * cols, cols), cols)

    def spread(source, slot):
        def one(step, carry):
            peer = lax.rem(me + step, seq)
            push(source(peer), col_in.at[slot, me], a_send.at[slot], a_recv.at[slot], (dp, peer))
            return carry

        lax.fori_loop(1, seq, one, 0)

    def arrived(slot):
        drain(col_in.at[slot, pl.ds(0, seq - 1)], a_recv.at[slot])

    def piece_cols(c):
        return pl.ds(pl.multiple_of(c * piece, piece), piece)

    near[0].wait()
    if inside:
        w_all[dp, z_at, y_at, core] = w_in[...]
        for c in range(CHUNKS):
            def z_step(step, carry, c=c):
                z_to = lax.rem(z_at + step, depth)
                block = w_all.at[dp, z_at, y_at, core, :, piece_cols(c)]
                push(block, block, g_send.at[0, c], g_recv.at[0, c],
                     (dp, (z_to * 2 + y_at) * 2 + core))
                return carry

            lax.fori_loop(1, depth, z_step, 0)
        weights = w_all
    else:
        weights = w_in

    row_at = lax.broadcasted_iota(jnp.int32, (tokens, tokens), 0)
    lane_at = lax.broadcasted_iota(jnp.int32, (tokens, tokens), 1)

    def moved(tensor, head_idx, forth):
        apart = (row_at - lane_at if forth else lane_at - row_at) - offset[head_idx]
        chosen = jnp.where((apart == 0) | (apart == -tokens), 1.0, 0.0).astype(BF16)
        return nn(chosen, tensor).astype(BF16)

    def move_all(tensor, src_slot):
        for head_idx in range(HC):
            shifted = moved(tensor[:, HALF + head_idx * HD:HALF + (head_idx + 1) * HD], head_idx, True)
            col_src[src_slot, :, :, head_idx * HD:(head_idx + 1) * HD] = shifted.reshape(seq, cols, HD)

    def spread_moved(src_slot, slot):
        spread(lambda peer: col_src.at[src_slot, peer], slot)
        col_in[slot, me] = col_src[src_slot, me]

    near[1].wait()
    move_all(k, 0)

    part_row = lax.broadcasted_iota(jnp.int32, (BLK, tokens), 0)
    part_lane = lax.broadcasted_iota(jnp.int32, (BLK, tokens), 1)
    col_bias[...] = jnp.where(lax.rem(part_row, cols) == lax.rem(part_lane, cols), 0.0, NEG)

    if inside:
        for c in range(CHUNKS):
            drain(w_all.at[0, pl.ds(0, depth - 1), 0, 0, :, piece_cols(c)], g_recv.at[0, c])
            block = w_all.at[dp, :, y_at, core, :, piece_cols(c)]
            push(block, block, g_send.at[1, c], g_recv.at[1, c],
                 (dp, (z_at * 2 + 1 - y_at) * 2 + core))
    near[2].wait()
    spread(lambda peer: q.at[col_rows(peer), pl.ds(HALF, HALF)], 0)
    col_in[0, me] = q[col_rows(me), HALF:]
    spread_moved(0, 1)
    near[3].wait()
    move_all(v, 1)
    if inside:
        for c in range(CHUNKS):
            drain(w_all.at[0, :, 0, 0, :, piece_cols(c)], g_recv.at[1, c])
            block = w_all.at[dp, :, :, core, :, piece_cols(c)]
            push(block, block, g_send.at[2, c], g_recv.at[2, c], (1 - dp, me))
    spread_moved(1, 2)
    if inside:
        for c in range(CHUNKS):
            drain(w_all.at[0, :, :, 0, :, piece_cols(c)], g_recv.at[2, c])
            block = w_all.at[:, :, :, core, :, piece_cols(c)]
            push(block, block, g_send.at[3, c], g_recv.at[3, c], (dp, pair * 2 + 1 - core))
        for c in range(CHUNKS):
            drain(w_all.at[:, :, :, 0, :, piece_cols(c)], g_recv.at[3, c])
    near[4].wait()

    tall = 256
    steps = tall // (4 * weights.shape[4])

    def attn_grad(half):
        def one(n, carry):
            rows = weights[half, pl.ds(n * steps, steps)].reshape(tall, width)
            part = nt(og[...], rows).astype(BF16)
            grads[:, pl.ds(pl.multiple_of(half * HALF + n * tall, tall), tall)] = part
            return carry

        lax.fori_loop(0, HALF // tall, one, 0)

    attn_grad(1)
    spread(lambda peer: grads.at[col_rows(peer), pl.ds(HALF, HALF)], 3)
    col_in[3, me] = grads[col_rows(me), HALF:]

    part_slots = BLK // cols

    def col_block(ref, slot, part, where):
        return ref[slot, part * part_slots:(part + 1) * part_slots, :, where].reshape(BLK, HD)

    def col_full(ref, slot, where):
        return ref[slot, :, :, where].reshape(tokens, HD)

    def col_put(slot, part, where, val):
        col_src[slot, part * part_slots:(part + 1) * part_slots, :, where] = (
            val.astype(BF16).reshape(part_slots, cols, HD))

    parts = tokens // BLK
    arrived(0)
    arrived(1)
    arrived(2)

    def col_forward(head_idx, carry):
        where = head_cols(head_idx)
        key, value = col_full(col_in, 1, where), col_full(col_in, 2, where)
        for part in range(parts):
            prob = probs(col_block(col_in, 0, part, where), key, col_bias[...])
            col_prob[head_idx, part * BLK:(part + 1) * BLK] = prob
            col_put(2, part, where, nn(prob.astype(BF16), value))
        return carry

    lax.fori_loop(0, HC, col_forward, 0)
    spread(lambda peer: col_src.at[2, peer], 4)
    col_in[4, me] = col_src[2, me]

    attn_grad(0)
    key_block = lax.broadcasted_iota(jnp.int32, (1, tokens), 1) // BLK

    def row_head(head_idx, carry):
        where = head_cols(head_idx)
        key, value = k[:, where], v[:, where]
        for part in range(parts):
            rows = slice(part * BLK, (part + 1) * BLK)
            seen = (key_block == part) | (key_block == pattern[head_idx, part])
            prob = probs(q[rows, where], key, jnp.where(seen, 0.0, NEG))
            half_prob = prob.astype(BF16)
            att[rows, where] = nn(half_prob, value).astype(BF16)
            score_grad = score_grads(prob, grads[rows, where], value)
            dq[rows, where] = (nn(score_grad, key) * SCALE).astype(BF16)
            p_scr[rows] = half_prob
            s_scr[rows] = score_grad
        dk[:, where] = (tn(s_scr[...], q[:, where]) * SCALE).astype(BF16)
        dv[:, where] = tn(p_scr[...], grads[:, where]).astype(BF16)
        return carry

    lax.fori_loop(0, HR // 2, row_head, 0)

    def w_part(half):
        att_t[...] = att[:, half * HALF:(half + 1) * HALF].astype(F32).T.astype(BF16)

        def one(c, carry):
            at = piece_cols(c)
            product = nn(att_t[...], og[:, at])
            if inside:
                wp[half, :, :, :, :, at] = product.astype(BF16).reshape(
                    depth, 2, 2, HALF // seq, piece)
                push(wp.at[half, :, :, 1 - core, :, at], core_in.at[half, :, :, :, at],
                     c_send.at[half, c], c_recv.at[half, c], (dp, pair * 2 + 1 - core))
            else:
                wg[pl.ds(half * HALF, HALF), at] = product
            return carry

        lax.fori_loop(0, CHUNKS, one, 0)

    def y_part(half):
        def one(c, carry):
            at = piece_cols(c)
            drain(core_in.at[half, :, :, :, at], c_recv.at[half, c])
            other = 1 - y_at
            y_src[half, :, :, at] = (
                wp[half, :, other, core, :, at].astype(F32) + core_in[half, :, other, :, at].astype(F32)
            ).astype(BF16)
            keep[half, :, :, at] = (
                wp[half, :, y_at, core, :, at].astype(F32) + core_in[half, :, y_at, :, at].astype(F32))
            push(y_src.at[half, :, :, at], y_in.at[half, :, :, at], y_send.at[half, c],
                 y_recv.at[half, c], (dp, (z_at * 2 + other) * 2 + core))
            return carry

        lax.fori_loop(0, CHUNKS, one, 0)

    arrived(3)

    def col_backward(head_idx, carry):
        where = head_cols(head_idx)
        key, value = col_full(col_in, 1, where), col_full(col_in, 2, where)
        for part in range(parts):
            rows = slice(part * BLK, (part + 1) * BLK)
            prob = col_prob[head_idx, rows]
            score_grad = score_grads(prob, col_block(col_in, 3, part, where), value)
            col_put(3, part, where, nn(score_grad, key) * SCALE)
            p_scr[rows] = prob.astype(BF16)
            s_scr[rows] = score_grad
        key_grad = tn(s_scr[...], col_full(col_in, 0, where)) * SCALE
        value_grad = tn(p_scr[...], col_full(col_in, 3, where))
        col_src[4, :, :, where] = key_grad.astype(BF16).reshape(seq, cols, HD)
        col_src[5, :, :, where] = value_grad.astype(BF16).reshape(seq, cols, HD)
        return carry

    lax.fori_loop(0, HC, col_backward, 0)

    for slot in (5, 6, 7):
        spread_moved(slot - 2, slot)
    lax.fori_loop(HR // 2, HR, row_head, 0)
    w_part(0)
    if inside:
        y_part(0)
    arrived(4)
    att[:, HALF:] = col_in[4].reshape(tokens, HALF)
    w_part(1)
    if inside:
        y_part(1)

        def x_step(c, carry):
            at = piece_cols(c)
            for half in (0, 1):
                drain(y_in.at[half, :, :, at], y_recv.at[half, c])
            x_src[:, :, at] = (
                keep[1 - dp, :, :, at] + y_in[1 - dp, :, :, at].astype(F32)).astype(BF16)
            push(x_src.at[:, :, at], x_in.at[:, :, at], x_send.at[c], x_recv.at[c], (1 - dp, me))
            return carry

        lax.fori_loop(0, CHUNKS, x_step, 0)

    def layer(n, carry):
        at = pl.ds(pl.multiple_of(n * tall, tall), tall)
        lo[:, at] = nn(att[...], weights[:, :, :, :, :, at].reshape(2 * HALF, tall)).astype(BF16)
        return carry

    lax.fori_loop(0, width // tall, layer, 0)

    if inside:
        def z_step(c, carry):
            at = piece_cols(c)
            drain(x_in.at[:, :, at], x_recv.at[c])
            z_src[:, :, at] = (
                keep[dp, :, :, at] + y_in[dp, :, :, at].astype(F32) + x_in[:, :, at].astype(F32)
            ).astype(BF16)
            z_in[z_at, :, at] = z_src[z_at, :, at]

            def one(step, inner):
                peer = lax.rem(z_at + step, depth)
                push(z_src.at[peer, :, at], z_in.at[z_at, :, at], z_send.at[c], z_recv.at[c],
                     (dp, (peer * 2 + y_at) * 2 + core))
                return inner

            lax.fori_loop(1, depth, one, 0)
            return carry

        lax.fori_loop(0, CHUNKS, z_step, 0)

    arrived(5)
    dq[:, HALF:] = col_in[5].reshape(tokens, HALF)
    for slot, target in ((6, dk), (7, dv)):
        arrived(slot)
        for head_idx in range(HC):
            lanes = slice(head_idx * HD, (head_idx + 1) * HD)
            back = moved(col_in[slot, :, :, lanes].reshape(tokens, HD), head_idx, False)
            target[:, HALF + head_idx * HD:HALF + (head_idx + 1) * HD] = back

    if inside:
        factor = (2 * seq * tokens) ** (-0.5)
        for c in range(CHUNKS):
            at = piece_cols(c)
            drain(z_in.at[pl.ds(0, depth - 1), :, at], z_recv.at[c])
            wg[:, at] = jnp.sum(z_in[:, :, at].astype(F32), axis=0) * factor
        for c in range(CHUNKS):
            drain(w_all.at[0, pl.ds(0, depth - 1), 0, 0, :, piece_cols(c)], g_send.at[0, c])
            drain(w_all.at[0, :, 0, 0, :, piece_cols(c)], g_send.at[1, c])
            drain(w_all.at[0, :, :, 0, :, piece_cols(c)], g_send.at[2, c])
            drain(w_all.at[:, :, :, 0, :, piece_cols(c)], g_send.at[3, c])
            for half in (0, 1):
                drain(core_in.at[half, :, :, :, piece_cols(c)], c_send.at[half, c])
                drain(y_in.at[half, :, :, piece_cols(c)], y_send.at[half, c])
            drain(x_in.at[:, :, piece_cols(c)], x_send.at[c])
            drain(z_in.at[pl.ds(0, depth - 1), :, piece_cols(c)], z_send.at[c])
    for slot in range(8):
        drain(col_in.at[slot, pl.ds(0, seq - 1)], a_send.at[slot])


def deliver(*refs):
    sources, targets, sem = refs[:5], refs[5:10], refs[10]
    copies = []
    for at, (source, target) in enumerate(zip(sources, targets)):
        cuts = 4 if source.shape[0] >= 64 else 1
        rows = source.shape[0] // cuts
        for cut in range(cuts):
            part = pl.ds(cut * rows, rows)
            copies.append(pltpu.make_async_copy(source.at[part], target.at[part], sem.at[at, cut]))
    for copy in copies:
        copy.start()
    for copy in copies:
        copy.wait()


def shards(dp_count, seq, queries, keys, values, out_proj, out_grad, block_pattern, col_offset):
    tokens, feats = queries.shape[2:]
    width = out_grad.shape[3]
    share = out_proj.shape[0]
    cols = tokens // seq
    inside = dp_count == 2 and share % 16 == 0
    split = (2, seq // 4, 2, 2, feats // (2 * seq), width)
    if inside:
        w_in = out_proj
    else:
        w_in = lax.all_gather(out_proj, ("dp", "seq"), axis=0, tiled=True).reshape(split)
    small = lambda shape, kind: pltpu.VMEM(shape if inside else (16, 128), kind)
    group = (seq // 4, share, width)
    sems = pltpu.SemaphoreType.DMA
    vmem = pl.BlockSpec(memory_space=pltpu.VMEM)
    smem = pl.BlockSpec(memory_space=pltpu.SMEM)
    flat = jax.ShapeDtypeStruct((tokens, feats), BF16)
    outs = pl.pallas_call(
        functools.partial(body, seq, inside),
        out_shape=[
            jax.ShapeDtypeStruct((tokens, width), BF16), flat, flat, flat,
            jax.ShapeDtypeStruct((share if inside else feats, width), F32),
        ],
        in_specs=[pl.BlockSpec(memory_space=pl.ANY)] * 5 + [smem] * 2,
        out_specs=[vmem] * 5,
        scratch_shapes=[
            pltpu.VMEM((tokens, feats), BF16),
            pltpu.VMEM((tokens, feats), BF16),
            pltpu.VMEM((tokens, feats), BF16),
            pltpu.VMEM(w_in.shape, BF16),
            pltpu.VMEM((tokens, width), BF16),
            sems((5,)),
            small(split, BF16),
            pltpu.VMEM((tokens, feats), BF16),
            pltpu.VMEM((tokens, feats), BF16),
            pltpu.VMEM((HALF, tokens), BF16),
            pltpu.VMEM((8, seq, cols, HALF), BF16),
            pltpu.VMEM((6, seq, cols, HALF), BF16),
            pltpu.VMEM((BLK, tokens), F32),
            pltpu.VMEM((HC, tokens, tokens), F32),
            pltpu.VMEM((tokens, tokens), BF16),
            pltpu.VMEM((tokens, tokens), BF16),
            small((2, seq // 4, 2, 2, share, width), BF16),
            small((2, seq // 4, 2, share, width), BF16),
            small((2,) + group, BF16),
            small((2,) + group, BF16),
            small((2,) + group, F32),
            small(group, BF16),
            small(group, BF16),
            small(group, BF16),
            small(group, BF16),
            sems((8,)), sems((8,)),
            sems((4, CHUNKS)), sems((4, CHUNKS)),
            sems((2, CHUNKS)), sems((2, CHUNKS)),
            sems((2, CHUNKS)), sems((2, CHUNKS)),
            sems((CHUNKS,)), sems((CHUNKS,)),
            sems((CHUNKS,)), sems((CHUNKS,)),
        ],
        compiler_params=pltpu.CompilerParams(
            collective_id=0, has_side_effects=True, vmem_limit_bytes=58 * 2 ** 20
        ),
        cost_estimate=pl.CostEstimate(
            flops=12 * 10 ** 9, bytes_accessed=11 * 2 ** 20, transcendentals=2 * 2 ** 20
        ),
    )(
        queries.reshape(tokens, feats), keys.reshape(tokens, feats), values.reshape(tokens, feats),
        w_in, out_grad.reshape(tokens, width), block_pattern, col_offset,
    )
    outs = pl.pallas_call(
        deliver,
        out_shape=[jax.ShapeDtypeStruct(out.shape, out.dtype) for out in outs],
        in_specs=[pl.BlockSpec(memory_space=pl.ANY)] * 5,
        out_specs=[pl.BlockSpec(memory_space=pl.ANY)] * 5,
        scratch_shapes=[sems((5, 4))],
        cost_estimate=pl.CostEstimate(flops=0, bytes_accessed=11 * 2 ** 20, transcendentals=0),
    )(*outs)
    layer_out, q_grad, k_grad, v_grad, w_grad = outs
    if not inside:
        w_grad = lax.psum_scatter(w_grad, ("dp", "seq"), scatter_dimension=0, tiled=True)
        w_grad = w_grad * (dp_count * seq * tokens) ** (-0.5)
    shape = (1, 1, tokens, feats)
    return (
        layer_out.reshape(1, 1, tokens, width),
        q_grad.reshape(shape), k_grad.reshape(shape), v_grad.reshape(shape), w_grad,
    )


def solution(mesh):
    rows = P("dp", "seq", None, None)
    flat = P(("dp", "seq"), None)
    in_specs = (rows, rows, rows, flat, rows, P(), P())
    out_specs = (rows, rows, rows, rows, flat)
    return jax.shard_map(
        functools.partial(shards, mesh.shape["dp"], mesh.shape["seq"]),
        mesh=mesh, in_specs=in_specs, out_specs=out_specs, check_vma=False,
    )
```

```python
import functools

import jax
import jax.numpy as jnp
from jax import lax
from jax.experimental import pallas as pl
from jax.experimental.pallas import tpu as pltpu
from jax.sharding import PartitionSpec as P

HD = 128
HR = 4
HC = 4
BLK = 128
NB = 4
HALF = HR * HD
CHUNKS = 4
SCALE = HD ** (-0.5)
NEG = -1e30
MESH = pl.DeviceIdType.MESH
F32 = jnp.float32
BF16 = jnp.bfloat16


def nt(a, b):
    return lax.dot_general(a, b, (((1,), (1,)), ((), ())), preferred_element_type=F32)


def nn(a, b):
    return jnp.dot(a, b, preferred_element_type=F32)


def tn(a, b):
    return lax.dot_general(a, b, (((0,), (0,)), ((), ())), preferred_element_type=F32)


def probs(query, key, bias):
    scores = nt(query, key) * SCALE + bias
    shifted = jnp.exp(scores - jnp.max(scores, axis=-1, keepdims=True))
    return shifted * (1.0 / jnp.sum(shifted, axis=-1, keepdims=True))


def score_grads(prob, grad, value):
    prob_grad = nt(grad, value)
    delta_sum = jnp.sum(prob * prob_grad, axis=-1, keepdims=True)
    return (prob * (prob_grad - delta_sum)).astype(BF16)


def head_cols(head_idx):
    return pl.ds(pl.multiple_of(head_idx * HD, HD), HD)


def body(seq, inside, q_far, k_far, v_far, w_far, og_far, pattern, offset, lo_far, dq_far, dk_far, dv_far, wg,
         q, k, v, w_in, og, l_sem, lo, row_grad, o_sem, w_all, grads, att, att_t, col_in, col_src, col_bias, col_prob, p_scr, s_scr,
         wp, core_in, y_src, y_in, keep, x_src, x_in, z_src, z_in,
         a_send, a_recv, g_send, g_recv, c_send, c_recv, y_send, y_recv, x_send, x_recv, z_send, z_recv):
    tokens = q.shape[0]
    cols = tokens // seq
    width = og.shape[1]
    piece = width // CHUNKS
    me = lax.axis_index("seq")
    dp = lax.axis_index("dp")
    core = lax.rem(me, 2)
    pair = me // 2
    y_at = lax.rem(pair, 2)
    z_at = pair // 2
    depth = seq // 4

    near = [pltpu.make_async_copy(far, close, l_sem.at[at]) for at, (far, close) in enumerate(
        ((w_far, w_in), (k_far, k), (q_far, q), (v_far, v), (og_far, og)))]
    for load in near:
        load.start()

    barrier = pltpu.get_barrier_semaphore()

    def greet(step, carry):
        pl.semaphore_signal(
            barrier, inc=1, device_id=(dp, lax.rem(me + step, seq)), device_id_type=MESH
        )
        return carry

    lax.fori_loop(1, seq, greet, 0)
    if inside:
        pl.semaphore_signal(barrier, inc=1, device_id=(1 - dp, me), device_id_type=MESH)
    pl.semaphore_wait(barrier, seq if inside else seq - 1)

    def push(src, dst, send, recv, target):
        pltpu.make_async_remote_copy(
            src_ref=src, dst_ref=dst, send_sem=send, recv_sem=recv,
            device_id=target, device_id_type=MESH,
        ).start()

    def drain(ref, sem):
        pltpu.make_async_copy(ref, ref, sem).wait()

    def col_rows(peer):
        return pl.ds(pl.multiple_of(peer * cols, cols), cols)

    def spread(source, slot):
        def one(step, carry):
            peer = lax.rem(me + step, seq)
            push(source(peer), col_in.at[slot, me], a_send.at[slot], a_recv.at[slot], (dp, peer))
            return carry

        lax.fori_loop(1, seq, one, 0)

    def arrived(slot):
        drain(col_in.at[slot, pl.ds(0, seq - 1)], a_recv.at[slot])

    def piece_cols(c):
        return pl.ds(pl.multiple_of(c * piece, piece), piece)

    near[0].wait()
    if inside:
        w_all[dp, z_at, y_at, core] = w_in[...]
        for c in range(CHUNKS):
            def z_step(step, carry, c=c):
                z_to = lax.rem(z_at + step, depth)
                block = w_all.at[dp, z_at, y_at, core, :, piece_cols(c)]
                push(block, block, g_send.at[0, c], g_recv.at[0, c],
                     (dp, (z_to * 2 + y_at) * 2 + core))
                return carry

            lax.fori_loop(1, depth, z_step, 0)
        weights = w_all
    else:
        weights = w_in

    row_at = lax.broadcasted_iota(jnp.int32, (tokens, tokens), 0)
    lane_at = lax.broadcasted_iota(jnp.int32, (tokens, tokens), 1)

    def moved(tensor, head_idx):
        apart = row_at - lane_at - offset[head_idx]
        chosen = jnp.where((apart == 0) | (apart == -tokens), 1.0, 0.0).astype(BF16)
        return nn(chosen, tensor).astype(BF16)

    def move_all(tensor, src_slot):
        for head_idx in range(HC):
            shifted = moved(tensor[:, HALF + head_idx * HD:HALF + (head_idx + 1) * HD], head_idx)
            col_src[src_slot, :, :, head_idx * HD:(head_idx + 1) * HD] = shifted.reshape(seq, cols, HD)

    def spread_moved(src_slot, slot):
        spread(lambda peer: col_src.at[src_slot, peer], slot)
        col_in[slot, me] = col_src[src_slot, me]

    near[1].wait()
    move_all(k, 0)

    part_row = lax.broadcasted_iota(jnp.int32, (BLK, tokens), 0)
    part_lane = lax.broadcasted_iota(jnp.int32, (BLK, tokens), 1)
    col_bias[...] = jnp.where(lax.rem(part_row, cols) == lax.rem(part_lane, cols), 0.0, NEG)

    if inside:
        for c in range(CHUNKS):
            drain(w_all.at[0, pl.ds(0, depth - 1), 0, 0, :, piece_cols(c)], g_recv.at[0, c])
            block = w_all.at[dp, :, y_at, core, :, piece_cols(c)]
            push(block, block, g_send.at[1, c], g_recv.at[1, c],
                 (dp, (z_at * 2 + 1 - y_at) * 2 + core))
    near[2].wait()
    spread(lambda peer: q.at[col_rows(peer), pl.ds(HALF, HALF)], 0)
    col_in[0, me] = q[col_rows(me), HALF:]
    spread_moved(0, 1)
    near[3].wait()
    move_all(v, 1)
    if inside:
        for c in range(CHUNKS):
            drain(w_all.at[0, :, 0, 0, :, piece_cols(c)], g_recv.at[1, c])
            block = w_all.at[dp, :, :, core, :, piece_cols(c)]
            push(block, block, g_send.at[2, c], g_recv.at[2, c], (1 - dp, me))
    spread_moved(1, 2)
    if inside:
        for c in range(CHUNKS):
            drain(w_all.at[0, :, :, 0, :, piece_cols(c)], g_recv.at[2, c])
            block = w_all.at[:, :, :, core, :, piece_cols(c)]
            push(block, block, g_send.at[3, c], g_recv.at[3, c], (dp, pair * 2 + 1 - core))
        for c in range(CHUNKS):
            drain(w_all.at[:, :, :, 0, :, piece_cols(c)], g_recv.at[3, c])
    near[4].wait()

    tall = 256
    steps = tall // (4 * weights.shape[4])

    def attn_grad(half):
        def one(n, carry):
            rows = weights[half, pl.ds(n * steps, steps)].reshape(tall, width)
            part = nt(og[...], rows).astype(BF16)
            grads[:, pl.ds(pl.multiple_of(half * HALF + n * tall, tall), tall)] = part
            return carry

        lax.fori_loop(0, HALF // tall, one, 0)

    attn_grad(1)
    spread(lambda peer: grads.at[col_rows(peer), pl.ds(HALF, HALF)], 3)
    col_in[3, me] = grads[col_rows(me), HALF:]

    part_slots = BLK // cols

    def col_block(ref, slot, part, where):
        return ref[slot, part * part_slots:(part + 1) * part_slots, :, where].reshape(BLK, HD)

    def col_full(ref, slot, where):
        return ref[slot, :, :, where].reshape(tokens, HD)

    def col_put(slot, part, where, val):
        col_src[slot, part * part_slots:(part + 1) * part_slots, :, where] = (
            val.astype(BF16).reshape(part_slots, cols, HD))

    parts = tokens // BLK
    arrived(0)
    arrived(1)
    arrived(2)

    def col_forward(head_idx, carry):
        where = head_cols(head_idx)
        key, value = col_full(col_in, 1, where), col_full(col_in, 2, where)
        for part in range(parts):
            prob = probs(col_block(col_in, 0, part, where), key, col_bias[...])
            col_prob[head_idx, part * BLK:(part + 1) * BLK] = prob
            col_put(2, part, where, nn(prob.astype(BF16), value))
        return carry

    lax.fori_loop(0, HC, col_forward, 0)
    spread(lambda peer: col_src.at[2, peer], 4)
    col_in[4, me] = col_src[2, me]

    attn_grad(0)
    key_block = lax.broadcasted_iota(jnp.int32, (1, tokens), 1) // BLK

    def row_head(head_idx, carry):
        where = head_cols(head_idx)
        key, value = k[:, where], v[:, where]
        for part in range(parts):
            rows = slice(part * BLK, (part + 1) * BLK)
            seen = (key_block == part) | (key_block == pattern[head_idx, part])
            prob = probs(q[rows, where], key, jnp.where(seen, 0.0, NEG))
            half_prob = prob.astype(BF16)
            att[rows, where] = nn(half_prob, value).astype(BF16)
            score_grad = score_grads(prob, grads[rows, where], value)
            row_grad[0, part * part_slots:(part + 1) * part_slots, :, where] = (
                (nn(score_grad, key) * SCALE).astype(BF16).reshape(part_slots, cols, HD))
            p_scr[rows] = half_prob
            s_scr[rows] = score_grad
        key_grad = (tn(s_scr[...], q[:, where]) * SCALE).astype(BF16)
        value_grad = tn(p_scr[...], grads[:, where]).astype(BF16)
        row_grad[1, :, :, where] = key_grad.reshape(seq, cols, HD)
        row_grad[2, :, :, where] = value_grad.reshape(seq, cols, HD)
        return carry

    def w_part(half):
        att_t[...] = att[:, half * HALF:(half + 1) * HALF].astype(F32).T.astype(BF16)

        def one(c, carry):
            at = piece_cols(c)
            product = nn(att_t[...], og[:, at])
            if inside:
                wp[half, :, :, :, :, at] = product.astype(BF16).reshape(
                    depth, 2, 2, HALF // seq, piece)
                push(wp.at[half, :, :, 1 - core, :, at], core_in.at[half, :, :, :, at],
                     c_send.at[half, c], c_recv.at[half, c], (dp, pair * 2 + 1 - core))
            else:
                wg[pl.ds(half * HALF, HALF), at] = product
            return carry

        lax.fori_loop(0, CHUNKS, one, 0)

    def y_part(half):
        def one(c, carry):
            at = piece_cols(c)
            drain(core_in.at[half, :, :, :, at], c_recv.at[half, c])
            other = 1 - y_at
            y_src[half, :, :, at] = (
                wp[half, :, other, core, :, at].astype(F32) + core_in[half, :, other, :, at].astype(F32)
            ).astype(BF16)
            keep[half, :, :, at] = (
                wp[half, :, y_at, core, :, at].astype(F32) + core_in[half, :, y_at, :, at].astype(F32))
            push(y_src.at[half, :, :, at], y_in.at[half, :, :, at], y_send.at[half, c],
                 y_recv.at[half, c], (dp, (z_at * 2 + other) * 2 + core))
            return carry

        lax.fori_loop(0, CHUNKS, one, 0)

    arrived(3)

    def col_backward(head_idx, carry):
        where = head_cols(head_idx)
        key, value = col_full(col_in, 1, where), col_full(col_in, 2, where)
        for part in range(parts):
            rows = slice(part * BLK, (part + 1) * BLK)
            prob = col_prob[head_idx, rows]
            score_grad = score_grads(prob, col_block(col_in, 3, part, where), value)
            col_put(3, part, where, nn(score_grad, key) * SCALE)
            p_scr[rows] = prob.astype(BF16)
            s_scr[rows] = score_grad
        key_grad = tn(s_scr[...], col_full(col_in, 0, where)) * SCALE
        value_grad = tn(p_scr[...], col_full(col_in, 3, where))
        col_src[4, :, :, where] = key_grad.astype(BF16).reshape(seq, cols, HD)
        col_src[5, :, :, where] = value_grad.astype(BF16).reshape(seq, cols, HD)

        def one(step, inner):
            peer = lax.rem(me + step, seq)
            push(col_src.at[pl.ds(3, 3), peer, :, where], col_in.at[pl.ds(5, 3), me, :, where],
                 a_send.at[5], a_recv.at[5], (dp, peer))
            return inner

        lax.fori_loop(1, seq, one, 0)
        return carry

    lax.fori_loop(0, HC, col_backward, 0)

    for slot in (5, 6, 7):
        col_in[slot, me] = col_src[slot - 2, me]
    arrived(4)
    att[:, HALF:] = col_in[4].reshape(tokens, HALF)
    w_part(1)
    lax.fori_loop(0, HR, row_head, 0)
    results = [
        pltpu.make_async_copy(row_grad.at[at], far.at[:, :, pl.ds(0, HALF)], o_sem.at[at])
        for at, far in enumerate((dq_far, dk_far, dv_far))]
    for result in results:
        result.start()
    if inside:
        y_part(1)
    w_part(0)
    if inside:
        y_part(0)

        def x_step(c, carry):
            at = piece_cols(c)
            for half in (0, 1):
                drain(y_in.at[half, :, :, at], y_recv.at[half, c])
            x_src[:, :, at] = (
                keep[1 - dp, :, :, at] + y_in[1 - dp, :, :, at].astype(F32)).astype(BF16)
            push(x_src.at[:, :, at], x_in.at[:, :, at], x_send.at[c], x_recv.at[c], (1 - dp, me))
            return carry

        lax.fori_loop(0, CHUNKS, x_step, 0)

    def layer(n, carry):
        at = pl.ds(pl.multiple_of(n * tall, tall), tall)
        lo[:, at] = nn(att[...], weights[:, :, :, :, :, at].reshape(2 * HALF, tall)).astype(BF16)
        return carry

    lax.fori_loop(0, width // tall, layer, 0)
    results.append(pltpu.make_async_copy(lo, lo_far, o_sem.at[6]))
    results[-1].start()

    if inside:
        def z_step(c, carry):
            at = piece_cols(c)
            drain(x_in.at[:, :, at], x_recv.at[c])
            z_src[:, :, at] = (
                keep[dp, :, :, at] + y_in[dp, :, :, at].astype(F32) + x_in[:, :, at].astype(F32)
            ).astype(BF16)
            z_in[z_at, :, at] = z_src[z_at, :, at]

            def one(step, inner):
                peer = lax.rem(z_at + step, depth)
                push(z_src.at[peer, :, at], z_in.at[z_at, :, at], z_send.at[c], z_recv.at[c],
                     (dp, (peer * 2 + y_at) * 2 + core))
                return inner

            lax.fori_loop(1, depth, one, 0)
            return carry

        lax.fori_loop(0, CHUNKS, z_step, 0)

    drain(col_in.at[pl.ds(5, 3), pl.ds(0, seq - 1)], a_recv.at[5])
    for at, far in enumerate((dq_far, dk_far, dv_far)):
        results.append(pltpu.make_async_copy(
            col_in.at[5 + at], far.at[:, :, pl.ds(HALF, HALF)], o_sem.at[3 + at]))
        results[-1].start()

    if inside:
        factor = (2 * seq * tokens) ** (-0.5)
        for c in range(CHUNKS):
            at = piece_cols(c)
            drain(z_in.at[pl.ds(0, depth - 1), :, at], z_recv.at[c])
            wg[:, at] = jnp.sum(z_in[:, :, at].astype(F32), axis=0) * factor
        for c in range(CHUNKS):
            drain(w_all.at[0, pl.ds(0, depth - 1), 0, 0, :, piece_cols(c)], g_send.at[0, c])
            drain(w_all.at[0, :, 0, 0, :, piece_cols(c)], g_send.at[1, c])
            drain(w_all.at[0, :, :, 0, :, piece_cols(c)], g_send.at[2, c])
            drain(w_all.at[:, :, :, 0, :, piece_cols(c)], g_send.at[3, c])
            for half in (0, 1):
                drain(core_in.at[half, :, :, :, piece_cols(c)], c_send.at[half, c])
                drain(y_in.at[half, :, :, piece_cols(c)], y_send.at[half, c])
            drain(x_in.at[:, :, piece_cols(c)], x_send.at[c])
            drain(z_in.at[pl.ds(0, depth - 1), :, piece_cols(c)], z_send.at[c])
    for slot in range(5):
        drain(col_in.at[slot, pl.ds(0, seq - 1)], a_send.at[slot])
    drain(col_in.at[pl.ds(5, 3), pl.ds(0, seq - 1)], a_send.at[5])
    for result in results:
        result.wait()


def deliver(offset, lo, dq, dk, dv, wg, lo_out, dq_out, dk_out, dv_out, wg_out):
    head_idx = pl.program_id(0)
    tokens = dk.shape[0]
    lo_out[...] = lo[...]
    dq_out[...] = dq[...]
    wg_out[...] = wg[...]

    @pl.when(head_idx < HR)
    def _():
        dk_out[...] = dk[...]
        dv_out[...] = dv[...]

    @pl.when(head_idx >= HR)
    def _():
        row_at = lax.broadcasted_iota(jnp.int32, (tokens, tokens), 0)
        lane_at = lax.broadcasted_iota(jnp.int32, (tokens, tokens), 1)
        apart = lane_at - row_at - offset[jnp.maximum(head_idx - HR, 0)]
        chosen = jnp.where((apart == 0) | (apart == -tokens), 1.0, 0.0).astype(BF16)
        dk_out[...] = nn(chosen, dk[...]).astype(BF16)
        dv_out[...] = nn(chosen, dv[...]).astype(BF16)


def shards(dp_count, seq, queries, keys, values, out_proj, out_grad, block_pattern, col_offset):
    tokens, feats = queries.shape[2:]
    width = out_grad.shape[3]
    share = out_proj.shape[0]
    cols = tokens // seq
    inside = dp_count == 2 and share % 16 == 0
    split = (2, seq // 4, 2, 2, feats // (2 * seq), width)
    if inside:
        w_in = out_proj
    else:
        w_in = lax.all_gather(out_proj, ("dp", "seq"), axis=0, tiled=True).reshape(split)
    small = lambda shape, kind: pltpu.VMEM(shape if inside else (16, 128), kind)
    group = (seq // 4, share, width)
    sems = pltpu.SemaphoreType.DMA
    vmem = pl.BlockSpec(memory_space=pltpu.VMEM)
    smem = pl.BlockSpec(memory_space=pltpu.SMEM)
    flat = jax.ShapeDtypeStruct((seq, cols, feats), BF16)
    outs = pl.pallas_call(
        functools.partial(body, seq, inside),
        out_shape=[
            jax.ShapeDtypeStruct((tokens, width), BF16), flat, flat, flat,
            jax.ShapeDtypeStruct((share if inside else feats, width), F32),
        ],
        in_specs=[pl.BlockSpec(memory_space=pl.ANY)] * 5 + [smem] * 2,
        out_specs=[pl.BlockSpec(memory_space=pl.ANY)] * 4 + [vmem],
        scratch_shapes=[
            pltpu.VMEM((tokens, feats), BF16),
            pltpu.VMEM((tokens, feats), BF16),
            pltpu.VMEM((tokens, feats), BF16),
            pltpu.VMEM(w_in.shape, BF16),
            pltpu.VMEM((tokens, width), BF16),
            sems((5,)),
            pltpu.VMEM((tokens, width), BF16),
            pltpu.VMEM((3, seq, cols, HALF), BF16),
            sems((7,)),
            small(split, BF16),
            pltpu.VMEM((tokens, feats), BF16),
            pltpu.VMEM((tokens, feats), BF16),
            pltpu.VMEM((HALF, tokens), BF16),
            pltpu.VMEM((8, seq, cols, HALF), BF16),
            pltpu.VMEM((6, seq, cols, HALF), BF16),
            pltpu.VMEM((BLK, tokens), F32),
            pltpu.VMEM((HC, tokens, tokens), F32),
            pltpu.VMEM((tokens, tokens), BF16),
            pltpu.VMEM((tokens, tokens), BF16),
            small((2, seq // 4, 2, 2, share, width), BF16),
            small((2, seq // 4, 2, share, width), BF16),
            small((2,) + group, BF16),
            small((2,) + group, BF16),
            small((2,) + group, F32),
            small(group, BF16),
            small(group, BF16),
            small(group, BF16),
            small(group, BF16),
            sems((6,)), sems((6,)),
            sems((4, CHUNKS)), sems((4, CHUNKS)),
            sems((2, CHUNKS)), sems((2, CHUNKS)),
            sems((2, CHUNKS)), sems((2, CHUNKS)),
            sems((CHUNKS,)), sems((CHUNKS,)),
            sems((CHUNKS,)), sems((CHUNKS,)),
        ],
        compiler_params=pltpu.CompilerParams(
            collective_id=0, has_side_effects=True, vmem_limit_bytes=58 * 2 ** 20
        ),
        cost_estimate=pl.CostEstimate(
            flops=12 * 10 ** 9, bytes_accessed=11 * 2 ** 20, transcendentals=2 * 2 ** 20
        ),
    )(
        queries.reshape(tokens, feats), keys.reshape(tokens, feats), values.reshape(tokens, feats),
        w_in, out_grad.reshape(tokens, width), block_pattern, col_offset,
    )
    outs = [outs[0]] + [out.reshape(tokens, feats) for out in outs[1:4]] + [outs[4]]
    lanes = [pl.BlockSpec((out.shape[0], out.shape[1] // (HR + HC)), lambda h: (0, h)) for out in outs]
    outs = pl.pallas_call(
        deliver,
        grid=(HR + HC,),
        out_shape=[jax.ShapeDtypeStruct(out.shape, out.dtype) for out in outs],
        in_specs=[smem] + lanes,
        out_specs=lanes,
        compiler_params=pltpu.CompilerParams(vmem_limit_bytes=32 * 2 ** 20),
        cost_estimate=pl.CostEstimate(
            flops=10 ** 9, bytes_accessed=11 * 2 ** 20, transcendentals=0
        ),
    )(col_offset, *outs)
    layer_out, q_grad, k_grad, v_grad, w_grad = outs
    if not inside:
        w_grad = lax.psum_scatter(w_grad, ("dp", "seq"), scatter_dimension=0, tiled=True)
        w_grad = w_grad * (dp_count * seq * tokens) ** (-0.5)
    shape = (1, 1, tokens, feats)
    return (
        layer_out.reshape(1, 1, tokens, width),
        q_grad.reshape(shape), k_grad.reshape(shape), v_grad.reshape(shape), w_grad,
    )


def solution(mesh):
    rows = P("dp", "seq", None, None)
    flat = P(("dp", "seq"), None)
    in_specs = (rows, rows, rows, flat, rows, P(), P())
    out_specs = (rows, rows, rows, rows, flat)
    return jax.shard_map(
        functools.partial(shards, mesh.shape["dp"], mesh.shape["seq"]),
        mesh=mesh, in_specs=in_specs, out_specs=out_specs, check_vma=False,
    )
```

```python
import functools

import jax
import jax.numpy as jnp
from jax import lax
from jax.experimental import pallas as pl
from jax.experimental.pallas import tpu as pltpu
from jax.sharding import PartitionSpec as P

HD = 128
HR = 4
HC = 4
BLK = 128
NB = 4
HALF = HR * HD
CHUNKS = 4
SCALE = HD ** (-0.5)
NEG = -1e30
MESH = pl.DeviceIdType.MESH
F32 = jnp.float32
BF16 = jnp.bfloat16


def nt(a, b):
    return lax.dot_general(a, b, (((1,), (1,)), ((), ())), preferred_element_type=F32)


def nn(a, b):
    return jnp.dot(a, b, preferred_element_type=F32)


def tn(a, b):
    return lax.dot_general(a, b, (((0,), (0,)), ((), ())), preferred_element_type=F32)


def probs(query, key, bias):
    scores = nt(query, key) * SCALE + bias
    shifted = jnp.exp(scores - jnp.max(scores, axis=-1, keepdims=True))
    return shifted * (1.0 / jnp.sum(shifted, axis=-1, keepdims=True))


def score_grads(prob, grad, value):
    prob_grad = nt(grad, value)
    delta_sum = jnp.sum(prob * prob_grad, axis=-1, keepdims=True)
    return (prob * (prob_grad - delta_sum)).astype(BF16)


def head_cols(head_idx):
    return pl.ds(pl.multiple_of(head_idx * HD, HD), HD)


def body(seq, inside, q_far, k_far, v_far, w_far, og_far, pattern, offset, lo_far, dq_far, dk_far, dv_far, wg,
         q, k, v, w_in, og, l_sem, lo, row_grad, o_sem, w_all, grads, att, att_t, col_in, col_src, col_bias, col_prob, p_scr, s_scr,
         wp, core_in, y_src, y_in, keep, x_src, x_in, z_src, z_in, z_keep, h_src, h_in,
         a_send, a_recv, g_send, g_recv, c_send, c_recv, y_send, y_recv, x_send, x_recv, z_send, z_recv):
    tokens = q.shape[0]
    cols = tokens // seq
    width = og.shape[1]
    piece = width // CHUNKS
    me = lax.axis_index("seq")
    dp = lax.axis_index("dp")
    core = lax.rem(me, 2)
    pair = me // 2
    y_at = lax.rem(pair, 2)
    z_at = pair // 2
    deep = seq // 8
    lo_at = lax.rem(z_at, 2)
    hi_at = z_at // 2

    def device(hi_to, lo_to, y_to, core_to):
        return (dp, ((hi_to * 2 + lo_to) * 2 + y_to) * 2 + core_to)

    near = [pltpu.make_async_copy(far, close, l_sem.at[at]) for at, (far, close) in enumerate(
        ((w_far, w_in), (k_far, k), (q_far, q), (v_far, v), (og_far, og)))]
    for load in near:
        load.start()

    barrier = pltpu.get_barrier_semaphore()

    def greet(step, carry):
        pl.semaphore_signal(
            barrier, inc=1, device_id=(dp, lax.rem(me + step, seq)), device_id_type=MESH
        )
        return carry

    lax.fori_loop(1, seq, greet, 0)
    if inside:
        pl.semaphore_signal(barrier, inc=1, device_id=(1 - dp, me), device_id_type=MESH)
    pl.semaphore_wait(barrier, seq if inside else seq - 1)

    def push(src, dst, send, recv, target):
        pltpu.make_async_remote_copy(
            src_ref=src, dst_ref=dst, send_sem=send, recv_sem=recv,
            device_id=target, device_id_type=MESH,
        ).start()

    def drain(ref, sem):
        pltpu.make_async_copy(ref, ref, sem).wait()

    def col_rows(peer):
        return pl.ds(pl.multiple_of(peer * cols, cols), cols)

    def spread(source, slot):
        def one(step, carry):
            peer = lax.rem(me + step, seq)
            push(source(peer), col_in.at[slot, me], a_send.at[slot], a_recv.at[slot], (dp, peer))
            return carry

        lax.fori_loop(1, seq, one, 0)

    def arrived(slot):
        drain(col_in.at[slot, pl.ds(0, seq - 1)], a_recv.at[slot])

    def piece_cols(c):
        return pl.ds(pl.multiple_of(c * piece, piece), piece)

    near[0].wait()
    if inside:
        w_all[dp, hi_at, lo_at, y_at, core] = w_in[...]
        for c in range(CHUNKS):
            block = w_all.at[dp, hi_at, lo_at, y_at, core, :, piece_cols(c)]
            push(block, block, g_send.at[4, c], g_recv.at[4, c], device(1 - hi_at, lo_at, y_at, core))
        for c in range(CHUNKS):
            drain(w_all.at[0, 0, 0, 0, 0, :, piece_cols(c)], g_recv.at[4, c])
            block = w_all.at[dp, :, lo_at, y_at, core, :, piece_cols(c)]
            push(block, block, g_send.at[0, c], g_recv.at[0, c], device(hi_at, 1 - lo_at, y_at, core))
        weights = w_all
    else:
        weights = w_in

    row_at = lax.broadcasted_iota(jnp.int32, (tokens, tokens), 0)
    lane_at = lax.broadcasted_iota(jnp.int32, (tokens, tokens), 1)

    def moved(tensor, head_idx):
        apart = row_at - lane_at - offset[head_idx]
        chosen = jnp.where((apart == 0) | (apart == -tokens), 1.0, 0.0).astype(BF16)
        return nn(chosen, tensor).astype(BF16)

    def move_all(tensor, src_slot):
        for head_idx in range(HC):
            shifted = moved(tensor[:, HALF + head_idx * HD:HALF + (head_idx + 1) * HD], head_idx)
            col_src[src_slot, :, :, head_idx * HD:(head_idx + 1) * HD] = shifted.reshape(seq, cols, HD)

    def spread_moved(src_slot, slot):
        spread(lambda peer: col_src.at[src_slot, peer], slot)
        col_in[slot, me] = col_src[src_slot, me]

    near[1].wait()
    move_all(k, 0)

    part_row = lax.broadcasted_iota(jnp.int32, (BLK, tokens), 0)
    part_lane = lax.broadcasted_iota(jnp.int32, (BLK, tokens), 1)
    col_bias[...] = jnp.where(lax.rem(part_row, cols) == lax.rem(part_lane, cols), 0.0, NEG)

    if inside:
        for c in range(CHUNKS):
            drain(w_all.at[0, :, 0, 0, 0, :, piece_cols(c)], g_recv.at[0, c])
            block = w_all.at[dp, :, :, y_at, core, :, piece_cols(c)]
            push(block, block, g_send.at[1, c], g_recv.at[1, c],
                 (dp, (z_at * 2 + 1 - y_at) * 2 + core))
    near[2].wait()
    spread(lambda peer: q.at[col_rows(peer), pl.ds(HALF, HALF)], 0)
    col_in[0, me] = q[col_rows(me), HALF:]
    spread_moved(0, 1)
    near[3].wait()
    move_all(v, 1)
    if inside:
        for c in range(CHUNKS):
            drain(w_all.at[0, :, :, 0, 0, :, piece_cols(c)], g_recv.at[1, c])
            block = w_all.at[dp, :, :, :, core, :, piece_cols(c)]
            push(block, block, g_send.at[2, c], g_recv.at[2, c], (1 - dp, me))
    spread_moved(1, 2)
    if inside:
        for c in range(CHUNKS):
            drain(w_all.at[0, :, :, :, 0, :, piece_cols(c)], g_recv.at[2, c])
            block = w_all.at[:, :, :, :, core, :, piece_cols(c)]
            push(block, block, g_send.at[3, c], g_recv.at[3, c], (dp, pair * 2 + 1 - core))
        for c in range(CHUNKS):
            drain(w_all.at[:, :, :, :, 0, :, piece_cols(c)], g_recv.at[3, c])
    near[4].wait()

    tall = 256
    steps = tall // (8 * weights.shape[5])

    def attn_grad(half):
        def one(n, carry):
            rows = weights[half, pl.ds(n * steps, steps)].reshape(tall, width)
            part = nt(og[...], rows).astype(BF16)
            grads[:, pl.ds(pl.multiple_of(half * HALF + n * tall, tall), tall)] = part
            return carry

        lax.fori_loop(0, HALF // tall, one, 0)

    attn_grad(1)
    spread(lambda peer: grads.at[col_rows(peer), pl.ds(HALF, HALF)], 3)
    col_in[3, me] = grads[col_rows(me), HALF:]

    part_slots = BLK // cols

    def col_block(ref, slot, part, where):
        return ref[slot, part * part_slots:(part + 1) * part_slots, :, where].reshape(BLK, HD)

    def col_full(ref, slot, where):
        return ref[slot, :, :, where].reshape(tokens, HD)

    def col_put(slot, part, where, val):
        col_src[slot, part * part_slots:(part + 1) * part_slots, :, where] = (
            val.astype(BF16).reshape(part_slots, cols, HD))

    parts = tokens // BLK
    arrived(0)
    arrived(1)
    arrived(2)

    def col_forward(head_idx, carry):
        where = head_cols(head_idx)
        key, value = col_full(col_in, 1, where), col_full(col_in, 2, where)
        for part in range(parts):
            prob = probs(col_block(col_in, 0, part, where), key, col_bias[...])
            col_prob[head_idx, part * BLK:(part + 1) * BLK] = prob
            col_put(2, part, where, nn(prob.astype(BF16), value))
        return carry

    lax.fori_loop(0, HC, col_forward, 0)
    spread(lambda peer: col_src.at[2, peer], 4)
    col_in[4, me] = col_src[2, me]

    attn_grad(0)
    key_block = lax.broadcasted_iota(jnp.int32, (1, tokens), 1) // BLK

    def row_head(head_idx, carry):
        where = head_cols(head_idx)
        key, value = k[:, where], v[:, where]
        for part in range(parts):
            rows = slice(part * BLK, (part + 1) * BLK)
            seen = (key_block == part) | (key_block == pattern[head_idx, part])
            prob = probs(q[rows, where], key, jnp.where(seen, 0.0, NEG))
            half_prob = prob.astype(BF16)
            att[rows, where] = nn(half_prob, value).astype(BF16)
            score_grad = score_grads(prob, grads[rows, where], value)
            row_grad[0, part * part_slots:(part + 1) * part_slots, :, where] = (
                (nn(score_grad, key) * SCALE).astype(BF16).reshape(part_slots, cols, HD))
            p_scr[rows] = half_prob
            s_scr[rows] = score_grad
        key_grad = (tn(s_scr[...], q[:, where]) * SCALE).astype(BF16)
        value_grad = tn(p_scr[...], grads[:, where]).astype(BF16)
        row_grad[1, :, :, where] = key_grad.reshape(seq, cols, HD)
        row_grad[2, :, :, where] = value_grad.reshape(seq, cols, HD)
        return carry

    def w_part(half):
        att_t[...] = att[:, half * HALF:(half + 1) * HALF].astype(F32).T.astype(BF16)

        def one(c, carry):
            at = piece_cols(c)
            product = nn(att_t[...], og[:, at])
            if inside:
                wp[half, :, :, :, :, :, at] = product.astype(BF16).reshape(
                    deep, 2, 2, 2, HALF // seq, piece)
                push(wp.at[half, :, :, :, 1 - core, :, at], core_in.at[half, :, :, :, :, at],
                     c_send.at[half, c], c_recv.at[half, c], device(hi_at, lo_at, y_at, 1 - core))
            else:
                wg[pl.ds(half * HALF, HALF), at] = product
            return carry

        lax.fori_loop(0, CHUNKS, one, 0)

    def y_part(half):
        def one(c, carry):
            at = piece_cols(c)
            drain(core_in.at[half, :, :, :, :, at], c_recv.at[half, c])
            other = 1 - y_at
            y_src[half, :, :, :, at] = (
                wp[half, :, :, other, core, :, at].astype(F32)
                + core_in[half, :, :, other, :, at].astype(F32)).astype(BF16)
            keep[half, :, :, :, at] = (
                wp[half, :, :, y_at, core, :, at].astype(F32)
                + core_in[half, :, :, y_at, :, at].astype(F32))
            push(y_src.at[half, :, :, :, at], y_in.at[half, :, :, :, at], y_send.at[half, c],
                 y_recv.at[half, c], device(hi_at, lo_at, other, core))
            return carry

        lax.fori_loop(0, CHUNKS, one, 0)

    arrived(3)

    def col_backward(head_idx, carry):
        where = head_cols(head_idx)
        key, value = col_full(col_in, 1, where), col_full(col_in, 2, where)
        for part in range(parts):
            rows = slice(part * BLK, (part + 1) * BLK)
            prob = col_prob[head_idx, rows]
            score_grad = score_grads(prob, col_block(col_in, 3, part, where), value)
            col_put(3, part, where, nn(score_grad, key) * SCALE)
            p_scr[rows] = prob.astype(BF16)
            s_scr[rows] = score_grad
        key_grad = tn(s_scr[...], col_full(col_in, 0, where)) * SCALE
        value_grad = tn(p_scr[...], col_full(col_in, 3, where))
        col_src[4, :, :, where] = key_grad.astype(BF16).reshape(seq, cols, HD)
        col_src[5, :, :, where] = value_grad.astype(BF16).reshape(seq, cols, HD)

        def one(step, inner):
            peer = lax.rem(me + step, seq)
            push(col_src.at[pl.ds(3, 3), peer, :, where], col_in.at[pl.ds(5, 3), me, :, where],
                 a_send.at[5], a_recv.at[5], (dp, peer))
            return inner

        lax.fori_loop(1, seq, one, 0)
        return carry

    lax.fori_loop(0, HC, col_backward, 0)

    for slot in (5, 6, 7):
        col_in[slot, me] = col_src[slot - 2, me]
    arrived(4)
    att[:, HALF:] = col_in[4].reshape(tokens, HALF)
    w_part(1)
    lax.fori_loop(0, HR, row_head, 0)
    results = [
        pltpu.make_async_copy(row_grad.at[at], far.at[:, :, pl.ds(0, HALF)], o_sem.at[at])
        for at, far in enumerate((dq_far, dk_far, dv_far))]
    for result in results:
        result.start()
    if inside:
        y_part(1)
    w_part(0)
    if inside:
        y_part(0)

        def x_step(c, carry):
            at = piece_cols(c)
            for half in (0, 1):
                drain(y_in.at[half, :, :, :, at], y_recv.at[half, c])
            x_src[:, :, :, at] = (
                keep[1 - dp, :, :, :, at] + y_in[1 - dp, :, :, :, at].astype(F32)).astype(BF16)
            push(x_src.at[:, :, :, at], x_in.at[:, :, :, at], x_send.at[c], x_recv.at[c], (1 - dp, me))
            return carry

        lax.fori_loop(0, CHUNKS, x_step, 0)

    def layer(n, carry):
        at = pl.ds(pl.multiple_of(n * tall, tall), tall)
        lo[:, at] = nn(att[...], weights[:, :, :, :, :, :, at].reshape(2 * HALF, tall)).astype(BF16)
        return carry

    lax.fori_loop(0, width // tall, layer, 0)
    results.append(pltpu.make_async_copy(lo, lo_far, o_sem.at[6]))
    results[-1].start()

    if inside:
        def z_step(c, carry):
            at = piece_cols(c)
            drain(x_in.at[:, :, :, at], x_recv.at[c])

            def total(which):
                return (keep[dp, :, which, :, at] + y_in[dp, :, which, :, at].astype(F32)
                        + x_in[:, which, :, at].astype(F32))

            z_src[:, :, at] = total(1 - lo_at).astype(BF16)
            z_keep[:, :, at] = total(lo_at)
            push(z_src.at[:, :, at], z_in.at[:, :, at], z_send.at[0, c], z_recv.at[0, c],
                 device(hi_at, 1 - lo_at, y_at, core))
            return carry

        lax.fori_loop(0, CHUNKS, z_step, 0)

        def h_step(c, carry):
            at = piece_cols(c)
            drain(z_in.at[:, :, at], z_recv.at[0, c])
            other = 1 - hi_at
            h_src[:, at] = (z_keep[other, :, at] + z_in[other, :, at].astype(F32)).astype(BF16)
            wg[:, at] = z_keep[hi_at, :, at] + z_in[hi_at, :, at].astype(F32)
            push(h_src.at[:, at], h_in.at[:, at], z_send.at[1, c], z_recv.at[1, c],
                 device(other, lo_at, y_at, core))
            return carry

        lax.fori_loop(0, CHUNKS, h_step, 0)

    drain(col_in.at[pl.ds(5, 3), pl.ds(0, seq - 1)], a_recv.at[5])
    for at, far in enumerate((dq_far, dk_far, dv_far)):
        results.append(pltpu.make_async_copy(
            col_in.at[5 + at], far.at[:, :, pl.ds(HALF, HALF)], o_sem.at[3 + at]))
        results[-1].start()

    if inside:
        factor = (2 * seq * tokens) ** (-0.5)
        for c in range(CHUNKS):
            at = piece_cols(c)
            drain(h_in.at[:, at], z_recv.at[1, c])
            wg[:, at] = (wg[:, at] + h_in[:, at].astype(F32)) * factor
        for c in range(CHUNKS):
            drain(w_all.at[0, :, 0, 0, 0, :, piece_cols(c)], g_send.at[0, c])
            drain(w_all.at[0, :, :, 0, 0, :, piece_cols(c)], g_send.at[1, c])
            drain(w_all.at[0, :, :, :, 0, :, piece_cols(c)], g_send.at[2, c])
            drain(w_all.at[:, :, :, :, 0, :, piece_cols(c)], g_send.at[3, c])
            for half in (0, 1):
                drain(core_in.at[half, :, :, :, :, piece_cols(c)], c_send.at[half, c])
                drain(y_in.at[half, :, :, :, piece_cols(c)], y_send.at[half, c])
            drain(x_in.at[:, :, :, piece_cols(c)], x_send.at[c])
            drain(z_in.at[:, :, piece_cols(c)], z_send.at[0, c])
            drain(h_in.at[:, piece_cols(c)], z_send.at[1, c])
            drain(w_all.at[0, 0, 0, 0, 0, :, piece_cols(c)], g_send.at[4, c])
    for slot in range(5):
        drain(col_in.at[slot, pl.ds(0, seq - 1)], a_send.at[slot])
    drain(col_in.at[pl.ds(5, 3), pl.ds(0, seq - 1)], a_send.at[5])
    for result in results:
        result.wait()


def deliver(offset, lo, dq, dk, dv, wg, lo_out, dq_out, dk_out, dv_out, wg_out):
    head_idx = pl.program_id(0)
    tokens = dk.shape[0]
    lo_out[...] = lo[...]
    dq_out[...] = dq[...]
    wg_out[...] = wg[...]

    @pl.when(head_idx < HR)
    def _():
        dk_out[...] = dk[...]
        dv_out[...] = dv[...]

    @pl.when(head_idx >= HR)
    def _():
        row_at = lax.broadcasted_iota(jnp.int32, (tokens, tokens), 0)
        lane_at = lax.broadcasted_iota(jnp.int32, (tokens, tokens), 1)
        apart = lane_at - row_at - offset[jnp.maximum(head_idx - HR, 0)]
        chosen = jnp.where((apart == 0) | (apart == -tokens), 1.0, 0.0).astype(BF16)
        dk_out[...] = nn(chosen, dk[...]).astype(BF16)
        dv_out[...] = nn(chosen, dv[...]).astype(BF16)


def shards(dp_count, seq, queries, keys, values, out_proj, out_grad, block_pattern, col_offset):
    tokens, feats = queries.shape[2:]
    width = out_grad.shape[3]
    share = out_proj.shape[0]
    cols = tokens // seq
    inside = dp_count == 2 and seq == 16 and share % 16 == 0
    split = (2, seq // 8, 2, 2, 2, feats // (2 * seq), width)
    if inside:
        w_in = out_proj
    else:
        w_in = lax.all_gather(out_proj, ("dp", "seq"), axis=0, tiled=True).reshape(split)
    small = lambda shape, kind: pltpu.VMEM(shape if inside else (16, 128), kind)
    group = (seq // 8, 2, share, width)
    sems = pltpu.SemaphoreType.DMA
    vmem = pl.BlockSpec(memory_space=pltpu.VMEM)
    smem = pl.BlockSpec(memory_space=pltpu.SMEM)
    flat = jax.ShapeDtypeStruct((seq, cols, feats), BF16)
    outs = pl.pallas_call(
        functools.partial(body, seq, inside),
        out_shape=[
            jax.ShapeDtypeStruct((tokens, width), BF16), flat, flat, flat,
            jax.ShapeDtypeStruct((share if inside else feats, width), F32),
        ],
        in_specs=[pl.BlockSpec(memory_space=pl.ANY)] * 5 + [smem] * 2,
        out_specs=[pl.BlockSpec(memory_space=pl.ANY)] * 4 + [vmem],
        scratch_shapes=[
            pltpu.VMEM((tokens, feats), BF16),
            pltpu.VMEM((tokens, feats), BF16),
            pltpu.VMEM((tokens, feats), BF16),
            pltpu.VMEM(w_in.shape, BF16),
            pltpu.VMEM((tokens, width), BF16),
            sems((5,)),
            pltpu.VMEM((tokens, width), BF16),
            pltpu.VMEM((3, seq, cols, HALF), BF16),
            sems((7,)),
            small(split, BF16),
            pltpu.VMEM((tokens, feats), BF16),
            pltpu.VMEM((tokens, feats), BF16),
            pltpu.VMEM((HALF, tokens), BF16),
            pltpu.VMEM((8, seq, cols, HALF), BF16),
            pltpu.VMEM((6, seq, cols, HALF), BF16),
            pltpu.VMEM((BLK, tokens), F32),
            pltpu.VMEM((HC, tokens, tokens), F32),
            pltpu.VMEM((tokens, tokens), BF16),
            pltpu.VMEM((tokens, tokens), BF16),
            small((2, seq // 8, 2, 2, 2, share, width), BF16),
            small((2, seq // 8, 2, 2, share, width), BF16),
            small((2,) + group, BF16),
            small((2,) + group, BF16),
            small((2,) + group, F32),
            small(group, BF16),
            small(group, BF16),
            small((2, share, width), BF16),
            small((2, share, width), BF16),
            small((2, share, width), F32),
            small((share, width), BF16),
            small((share, width), BF16),
            sems((6,)), sems((6,)),
            sems((5, CHUNKS)), sems((5, CHUNKS)),
            sems((2, CHUNKS)), sems((2, CHUNKS)),
            sems((2, CHUNKS)), sems((2, CHUNKS)),
            sems((CHUNKS,)), sems((CHUNKS,)),
            sems((2, CHUNKS)), sems((2, CHUNKS)),
        ],
        compiler_params=pltpu.CompilerParams(
            collective_id=0, has_side_effects=True, vmem_limit_bytes=58 * 2 ** 20
        ),
        cost_estimate=pl.CostEstimate(
            flops=12 * 10 ** 9, bytes_accessed=11 * 2 ** 20, transcendentals=2 * 2 ** 20
        ),
    )(
        queries.reshape(tokens, feats), keys.reshape(tokens, feats), values.reshape(tokens, feats),
        w_in, out_grad.reshape(tokens, width), block_pattern, col_offset,
    )
    outs = [outs[0]] + [out.reshape(tokens, feats) for out in outs[1:4]] + [outs[4]]
    lanes = [pl.BlockSpec((out.shape[0], out.shape[1] // (HR + HC)), lambda h: (0, h)) for out in outs]
    outs = pl.pallas_call(
        deliver,
        grid=(HR + HC,),
        out_shape=[jax.ShapeDtypeStruct(out.shape, out.dtype) for out in outs],
        in_specs=[smem] + lanes,
        out_specs=lanes,
        compiler_params=pltpu.CompilerParams(vmem_limit_bytes=60 * 2 ** 20),
        cost_estimate=pl.CostEstimate(
            flops=10 ** 9, bytes_accessed=11 * 2 ** 20, transcendentals=0
        ),
    )(col_offset, *outs)
    layer_out, q_grad, k_grad, v_grad, w_grad = outs
    if not inside:
        w_grad = lax.psum_scatter(w_grad, ("dp", "seq"), scatter_dimension=0, tiled=True)
        w_grad = w_grad * (dp_count * seq * tokens) ** (-0.5)
    shape = (1, 1, tokens, feats)
    return (
        layer_out.reshape(1, 1, tokens, width),
        q_grad.reshape(shape), k_grad.reshape(shape), v_grad.reshape(shape), w_grad,
    )


def solution(mesh):
    rows = P("dp", "seq", None, None)
    flat = P(("dp", "seq"), None)
    in_specs = (rows, rows, rows, flat, rows, P(), P())
    out_specs = (rows, rows, rows, rows, flat)
    return jax.shard_map(
        functools.partial(shards, mesh.shape["dp"], mesh.shape["seq"]),
        mesh=mesh, in_specs=in_specs, out_specs=out_specs, check_vma=False,
    )
```

```python
import functools

import jax
import jax.numpy as jnp
from jax import lax
from jax.experimental import pallas as pl
from jax.experimental.pallas import tpu as pltpu
from jax.sharding import PartitionSpec as P

HD = 128
HR = 4
HC = 4
BLK = 128
NB = 4
HALF = HR * HD
CHUNKS = 4
SCALE = HD ** (-0.5)
NEG = -1e30
MESH = pl.DeviceIdType.MESH
F32 = jnp.float32
BF16 = jnp.bfloat16


def nt(a, b):
    return lax.dot_general(a, b, (((1,), (1,)), ((), ())), preferred_element_type=F32)


def nn(a, b):
    return jnp.dot(a, b, preferred_element_type=F32)


def tn(a, b):
    return lax.dot_general(a, b, (((0,), (0,)), ((), ())), preferred_element_type=F32)


def probs(query, key, bias):
    scores = nt(query, key) * SCALE + bias
    shifted = jnp.exp(scores - jnp.max(scores, axis=-1, keepdims=True))
    return shifted * (1.0 / jnp.sum(shifted, axis=-1, keepdims=True))


def score_grads(prob, grad, value):
    prob_grad = nt(grad, value)
    delta_sum = jnp.sum(prob * prob_grad, axis=-1, keepdims=True)
    return (prob * (prob_grad - delta_sum)).astype(BF16)


def head_cols(head_idx):
    return pl.ds(pl.multiple_of(head_idx * HD, HD), HD)


def body(seq, inside, q_far, k_far, v_far, w_far, og_far, pattern, offset, lo_far, dq_far, dk_far, dv_far, wg,
         q, k, v, w_in, og, l_sem, lo, row_grad, back, o_sem, w_all, grads, att, att_t, col_in, col_src, col_bias, col_prob, p_scr, s_scr,
         wp, core_in, y_src, y_in, keep, x_src, x_in, z_src, z_in, z_keep, h_src, h_in,
         a_send, a_recv, g_send, g_recv, c_send, c_recv, y_send, y_recv, x_send, x_recv, z_send, z_recv):
    tokens = q.shape[0]
    cols = tokens // seq
    width = og.shape[1]
    piece = width // CHUNKS
    me = lax.axis_index("seq")
    dp = lax.axis_index("dp")
    core = lax.rem(me, 2)
    pair = me // 2
    y_at = lax.rem(pair, 2)
    z_at = pair // 2
    deep = seq // 8
    lo_at = lax.rem(z_at, 2)
    hi_at = z_at // 2

    def device(hi_to, lo_to, y_to, core_to):
        return (dp, ((hi_to * 2 + lo_to) * 2 + y_to) * 2 + core_to)

    near = [pltpu.make_async_copy(far, close, l_sem.at[at]) for at, (far, close) in enumerate(
        ((w_far, w_in), (k_far, k), (q_far, q), (v_far, v), (og_far, og)))]
    for load in near:
        load.start()

    barrier = pltpu.get_barrier_semaphore()

    def greet(step, carry):
        pl.semaphore_signal(
            barrier, inc=1, device_id=(dp, lax.rem(me + step, seq)), device_id_type=MESH
        )
        return carry

    lax.fori_loop(1, seq, greet, 0)
    if inside:
        pl.semaphore_signal(barrier, inc=1, device_id=(1 - dp, me), device_id_type=MESH)
    pl.semaphore_wait(barrier, seq if inside else seq - 1)

    def push(src, dst, send, recv, target):
        pltpu.make_async_remote_copy(
            src_ref=src, dst_ref=dst, send_sem=send, recv_sem=recv,
            device_id=target, device_id_type=MESH,
        ).start()

    def drain(ref, sem):
        pltpu.make_async_copy(ref, ref, sem).wait()

    def col_rows(peer):
        return pl.ds(pl.multiple_of(peer * cols, cols), cols)

    def spread(source, slot):
        def one(step, carry):
            peer = lax.rem(me + step, seq)
            push(source(peer), col_in.at[slot, me], a_send.at[slot], a_recv.at[slot], (dp, peer))
            return carry

        lax.fori_loop(1, seq, one, 0)

    def arrived(slot):
        drain(col_in.at[slot, pl.ds(0, seq - 1)], a_recv.at[slot])

    def piece_cols(c):
        return pl.ds(pl.multiple_of(c * piece, piece), piece)

    near[0].wait()
    if inside:
        w_all[dp, hi_at, lo_at, y_at, core] = w_in[...]
        for c in range(CHUNKS):
            block = w_all.at[dp, hi_at, lo_at, y_at, core, :, piece_cols(c)]
            push(block, block, g_send.at[4, c], g_recv.at[4, c], device(1 - hi_at, lo_at, y_at, core))
        for c in range(CHUNKS):
            drain(w_all.at[0, 0, 0, 0, 0, :, piece_cols(c)], g_recv.at[4, c])
            block = w_all.at[dp, :, lo_at, y_at, core, :, piece_cols(c)]
            push(block, block, g_send.at[0, c], g_recv.at[0, c], device(hi_at, 1 - lo_at, y_at, core))
        weights = w_all
    else:
        weights = w_in

    row_at = lax.broadcasted_iota(jnp.int32, (tokens, tokens), 0)
    lane_at = lax.broadcasted_iota(jnp.int32, (tokens, tokens), 1)

    def moved(tensor, head_idx, forth):
        apart = (row_at - lane_at if forth else lane_at - row_at) - offset[head_idx]
        chosen = jnp.where((apart == 0) | (apart == -tokens), 1.0, 0.0).astype(BF16)
        return nn(chosen, tensor).astype(BF16)

    def move_all(tensor, src_slot):
        for head_idx in range(HC):
            shifted = moved(tensor[:, HALF + head_idx * HD:HALF + (head_idx + 1) * HD], head_idx, True)
            col_src[src_slot, :, :, head_idx * HD:(head_idx + 1) * HD] = shifted.reshape(seq, cols, HD)

    def spread_moved(src_slot, slot):
        spread(lambda peer: col_src.at[src_slot, peer], slot)
        col_in[slot, me] = col_src[src_slot, me]

    near[1].wait()
    move_all(k, 0)

    part_row = lax.broadcasted_iota(jnp.int32, (BLK, tokens), 0)
    part_lane = lax.broadcasted_iota(jnp.int32, (BLK, tokens), 1)
    col_bias[...] = jnp.where(lax.rem(part_row, cols) == lax.rem(part_lane, cols), 0.0, NEG)

    if inside:
        for c in range(CHUNKS):
            drain(w_all.at[0, :, 0, 0, 0, :, piece_cols(c)], g_recv.at[0, c])
            block = w_all.at[dp, :, :, y_at, core, :, piece_cols(c)]
            push(block, block, g_send.at[1, c], g_recv.at[1, c],
                 (dp, (z_at * 2 + 1 - y_at) * 2 + core))
    near[2].wait()
    spread(lambda peer: q.at[col_rows(peer), pl.ds(HALF, HALF)], 0)
    col_in[0, me] = q[col_rows(me), HALF:]
    spread_moved(0, 1)
    near[3].wait()
    move_all(v, 1)
    if inside:
        for c in range(CHUNKS):
            drain(w_all.at[0, :, :, 0, 0, :, piece_cols(c)], g_recv.at[1, c])
            block = w_all.at[dp, :, :, :, core, :, piece_cols(c)]
            push(block, block, g_send.at[2, c], g_recv.at[2, c], (1 - dp, me))
    spread_moved(1, 2)
    if inside:
        for c in range(CHUNKS):
            drain(w_all.at[0, :, :, :, 0, :, piece_cols(c)], g_recv.at[2, c])
            block = w_all.at[:, :, :, :, core, :, piece_cols(c)]
            push(block, block, g_send.at[3, c], g_recv.at[3, c], (dp, pair * 2 + 1 - core))
        for c in range(CHUNKS):
            drain(w_all.at[:, :, :, :, 0, :, piece_cols(c)], g_recv.at[3, c])
    near[4].wait()

    tall = 256
    steps = tall // (8 * weights.shape[5])

    def attn_grad(half):
        def one(n, carry):
            rows = weights[half, pl.ds(n * steps, steps)].reshape(tall, width)
            part = nt(og[...], rows).astype(BF16)
            grads[:, pl.ds(pl.multiple_of(half * HALF + n * tall, tall), tall)] = part
            return carry

        lax.fori_loop(0, HALF // tall, one, 0)

    attn_grad(1)
    spread(lambda peer: grads.at[col_rows(peer), pl.ds(HALF, HALF)], 3)
    col_in[3, me] = grads[col_rows(me), HALF:]

    part_slots = BLK // cols

    def col_block(ref, slot, part, where):
        return ref[slot, part * part_slots:(part + 1) * part_slots, :, where].reshape(BLK, HD)

    def col_full(ref, slot, where):
        return ref[slot, :, :, where].reshape(tokens, HD)

    def col_put(slot, part, where, val):
        col_src[slot, part * part_slots:(part + 1) * part_slots, :, where] = (
            val.astype(BF16).reshape(part_slots, cols, HD))

    parts = tokens // BLK
    arrived(0)
    arrived(1)
    arrived(2)

    def col_forward(head_idx, carry):
        where = head_cols(head_idx)
        key, value = col_full(col_in, 1, where), col_full(col_in, 2, where)
        for part in range(parts):
            prob = probs(col_block(col_in, 0, part, where), key, col_bias[...])
            col_prob[head_idx, part * BLK:(part + 1) * BLK] = prob
            col_put(2, part, where, nn(prob.astype(BF16), value))
        return carry

    lax.fori_loop(0, HC, col_forward, 0)
    spread(lambda peer: col_src.at[2, peer], 4)
    col_in[4, me] = col_src[2, me]

    attn_grad(0)
    key_block = lax.broadcasted_iota(jnp.int32, (1, tokens), 1) // BLK

    def row_head(head_idx, carry):
        where = head_cols(head_idx)
        key, value = k[:, where], v[:, where]
        for part in range(parts):
            rows = slice(part * BLK, (part + 1) * BLK)
            seen = (key_block == part) | (key_block == pattern[head_idx, part])
            prob = probs(q[rows, where], key, jnp.where(seen, 0.0, NEG))
            half_prob = prob.astype(BF16)
            att[rows, where] = nn(half_prob, value).astype(BF16)
            score_grad = score_grads(prob, grads[rows, where], value)
            row_grad[0, part * part_slots:(part + 1) * part_slots, :, where] = (
                (nn(score_grad, key) * SCALE).astype(BF16).reshape(part_slots, cols, HD))
            p_scr[rows] = half_prob
            s_scr[rows] = score_grad
        key_grad = (tn(s_scr[...], q[:, where]) * SCALE).astype(BF16)
        value_grad = tn(p_scr[...], grads[:, where]).astype(BF16)
        row_grad[1, :, :, where] = key_grad.reshape(seq, cols, HD)
        row_grad[2, :, :, where] = value_grad.reshape(seq, cols, HD)
        return carry

    def w_part(half):
        att_t[...] = att[:, half * HALF:(half + 1) * HALF].astype(F32).T.astype(BF16)

        def one(c, carry):
            at = piece_cols(c)
            product = nn(att_t[...], og[:, at])
            if inside:
                wp[half, :, :, :, :, :, at] = product.astype(BF16).reshape(
                    deep, 2, 2, 2, HALF // seq, piece)
                push(wp.at[half, :, :, :, 1 - core, :, at], core_in.at[half, :, :, :, :, at],
                     c_send.at[half, c], c_recv.at[half, c], device(hi_at, lo_at, y_at, 1 - core))
            else:
                wg[pl.ds(half * HALF, HALF), at] = product
            return carry

        lax.fori_loop(0, CHUNKS, one, 0)

    def y_part(half):
        def one(c, carry):
            at = piece_cols(c)
            drain(core_in.at[half, :, :, :, :, at], c_recv.at[half, c])
            other = 1 - y_at
            y_src[half, :, :, :, at] = (
                wp[half, :, :, other, core, :, at].astype(F32)
                + core_in[half, :, :, other, :, at].astype(F32)).astype(BF16)
            keep[half, :, :, :, at] = (
                wp[half, :, :, y_at, core, :, at].astype(F32)
                + core_in[half, :, :, y_at, :, at].astype(F32))
            push(y_src.at[half, :, :, :, at], y_in.at[half, :, :, :, at], y_send.at[half, c],
                 y_recv.at[half, c], device(hi_at, lo_at, other, core))
            return carry

        lax.fori_loop(0, CHUNKS, one, 0)

    arrived(3)

    def col_backward(head_idx, carry):
        where = head_cols(head_idx)
        key, value = col_full(col_in, 1, where), col_full(col_in, 2, where)
        for part in range(parts):
            rows = slice(part * BLK, (part + 1) * BLK)
            prob = col_prob[head_idx, rows]
            score_grad = score_grads(prob, col_block(col_in, 3, part, where), value)
            col_put(3, part, where, nn(score_grad, key) * SCALE)
            p_scr[rows] = prob.astype(BF16)
            s_scr[rows] = score_grad
        key_grad = tn(s_scr[...], col_full(col_in, 0, where)) * SCALE
        value_grad = tn(p_scr[...], col_full(col_in, 3, where))
        col_src[4, :, :, where] = key_grad.astype(BF16).reshape(seq, cols, HD)
        col_src[5, :, :, where] = value_grad.astype(BF16).reshape(seq, cols, HD)

        def one(step, inner):
            peer = lax.rem(me + step, seq)
            push(col_src.at[pl.ds(3, 3), peer, :, where], col_in.at[pl.ds(5, 3), me, :, where],
                 a_send.at[5], a_recv.at[5], (dp, peer))
            return inner

        lax.fori_loop(1, seq, one, 0)
        return carry

    lax.fori_loop(0, HC, col_backward, 0)

    for slot in (5, 6, 7):
        col_in[slot, me] = col_src[slot - 2, me]
    arrived(4)
    att[:, HALF:] = col_in[4].reshape(tokens, HALF)
    w_part(1)
    lax.fori_loop(0, HR, row_head, 0)
    results = [
        pltpu.make_async_copy(row_grad.at[at], far.at[:, :, pl.ds(0, HALF)], o_sem.at[at])
        for at, far in enumerate((dq_far, dk_far, dv_far))]
    for result in results:
        result.start()
    if inside:
        y_part(1)
    w_part(0)
    if inside:
        y_part(0)

        def x_step(c, carry):
            at = piece_cols(c)
            for half in (0, 1):
                drain(y_in.at[half, :, :, :, at], y_recv.at[half, c])
            x_src[:, :, :, at] = (
                keep[1 - dp, :, :, :, at] + y_in[1 - dp, :, :, :, at].astype(F32)).astype(BF16)
            push(x_src.at[:, :, :, at], x_in.at[:, :, :, at], x_send.at[c], x_recv.at[c], (1 - dp, me))
            return carry

        lax.fori_loop(0, CHUNKS, x_step, 0)

    def layer(n, carry):
        at = pl.ds(pl.multiple_of(n * tall, tall), tall)
        lo[:, at] = nn(att[...], weights[:, :, :, :, :, :, at].reshape(2 * HALF, tall)).astype(BF16)
        return carry

    lax.fori_loop(0, width // tall, layer, 0)
    results.append(pltpu.make_async_copy(lo, lo_far, o_sem.at[6]))
    results[-1].start()

    if inside:
        def z_step(c, carry):
            at = piece_cols(c)
            drain(x_in.at[:, :, :, at], x_recv.at[c])

            def total(which):
                return (keep[dp, :, which, :, at] + y_in[dp, :, which, :, at].astype(F32)
                        + x_in[:, which, :, at].astype(F32))

            z_src[:, :, at] = total(1 - lo_at).astype(BF16)
            z_keep[:, :, at] = total(lo_at)
            push(z_src.at[:, :, at], z_in.at[:, :, at], z_send.at[0, c], z_recv.at[0, c],
                 device(hi_at, 1 - lo_at, y_at, core))
            return carry

        lax.fori_loop(0, CHUNKS, z_step, 0)

        def h_step(c, carry):
            at = piece_cols(c)
            drain(z_in.at[:, :, at], z_recv.at[0, c])
            other = 1 - hi_at
            h_src[:, at] = (z_keep[other, :, at] + z_in[other, :, at].astype(F32)).astype(BF16)
            wg[:, at] = z_keep[hi_at, :, at] + z_in[hi_at, :, at].astype(F32)
            push(h_src.at[:, at], h_in.at[:, at], z_send.at[1, c], z_recv.at[1, c],
                 device(other, lo_at, y_at, core))
            return carry

        lax.fori_loop(0, CHUNKS, h_step, 0)

    drain(col_in.at[pl.ds(5, 3), pl.ds(0, seq - 1)], a_recv.at[5])
    for at, far in enumerate((dq_far, dk_far, dv_far)):
        if at > 0:
            for head_idx in range(HC):
                lanes = slice(head_idx * HD, (head_idx + 1) * HD)
                home = moved(col_in[5 + at, :, :, lanes].reshape(tokens, HD), head_idx, False)
                back[at - 1, :, :, lanes] = home.reshape(seq, cols, HD)
        results.append(pltpu.make_async_copy(
            back.at[at - 1] if at > 0 else col_in.at[5],
            far.at[:, :, pl.ds(HALF, HALF)], o_sem.at[3 + at]))
        results[-1].start()

    if inside:
        factor = (2 * seq * tokens) ** (-0.5)
        for c in range(CHUNKS):
            at = piece_cols(c)
            drain(h_in.at[:, at], z_recv.at[1, c])
            wg[:, at] = (wg[:, at] + h_in[:, at].astype(F32)) * factor
        for c in range(CHUNKS):
            drain(w_all.at[0, :, 0, 0, 0, :, piece_cols(c)], g_send.at[0, c])
            drain(w_all.at[0, :, :, 0, 0, :, piece_cols(c)], g_send.at[1, c])
            drain(w_all.at[0, :, :, :, 0, :, piece_cols(c)], g_send.at[2, c])
            drain(w_all.at[:, :, :, :, 0, :, piece_cols(c)], g_send.at[3, c])
            for half in (0, 1):
                drain(core_in.at[half, :, :, :, :, piece_cols(c)], c_send.at[half, c])
                drain(y_in.at[half, :, :, :, piece_cols(c)], y_send.at[half, c])
            drain(x_in.at[:, :, :, piece_cols(c)], x_send.at[c])
            drain(z_in.at[:, :, piece_cols(c)], z_send.at[0, c])
            drain(h_in.at[:, piece_cols(c)], z_send.at[1, c])
            drain(w_all.at[0, 0, 0, 0, 0, :, piece_cols(c)], g_send.at[4, c])
    for slot in range(5):
        drain(col_in.at[slot, pl.ds(0, seq - 1)], a_send.at[slot])
    drain(col_in.at[pl.ds(5, 3), pl.ds(0, seq - 1)], a_send.at[5])
    for result in results:
        result.wait()


def deliver(*refs):
    for source, target in zip(refs[:5], refs[5:]):
        target[...] = source[...]


def shards(dp_count, seq, queries, keys, values, out_proj, out_grad, block_pattern, col_offset):
    tokens, feats = queries.shape[2:]
    width = out_grad.shape[3]
    share = out_proj.shape[0]
    cols = tokens // seq
    inside = dp_count == 2 and seq == 16 and share % 16 == 0
    split = (2, seq // 8, 2, 2, 2, feats // (2 * seq), width)
    if inside:
        w_in = out_proj
    else:
        w_in = lax.all_gather(out_proj, ("dp", "seq"), axis=0, tiled=True).reshape(split)
    small = lambda shape, kind: pltpu.VMEM(shape if inside else (16, 128), kind)
    group = (seq // 8, 2, share, width)
    sems = pltpu.SemaphoreType.DMA
    vmem = pl.BlockSpec(memory_space=pltpu.VMEM)
    smem = pl.BlockSpec(memory_space=pltpu.SMEM)
    flat = jax.ShapeDtypeStruct((seq, cols, feats), BF16)
    outs = pl.pallas_call(
        functools.partial(body, seq, inside),
        out_shape=[
            jax.ShapeDtypeStruct((tokens, width), BF16), flat, flat, flat,
            jax.ShapeDtypeStruct((share if inside else feats, width), F32),
        ],
        in_specs=[pl.BlockSpec(memory_space=pl.ANY)] * 5 + [smem] * 2,
        out_specs=[pl.BlockSpec(memory_space=pl.ANY)] * 4 + [vmem],
        scratch_shapes=[
            pltpu.VMEM((tokens, feats), BF16),
            pltpu.VMEM((tokens, feats), BF16),
            pltpu.VMEM((tokens, feats), BF16),
            pltpu.VMEM(w_in.shape, BF16),
            pltpu.VMEM((tokens, width), BF16),
            sems((5,)),
            pltpu.VMEM((tokens, width), BF16),
            pltpu.VMEM((3, seq, cols, HALF), BF16),
            pltpu.VMEM((2, seq, cols, HALF), BF16),
            sems((7,)),
            small(split, BF16),
            pltpu.VMEM((tokens, feats), BF16),
            pltpu.VMEM((tokens, feats), BF16),
            pltpu.VMEM((HALF, tokens), BF16),
            pltpu.VMEM((8, seq, cols, HALF), BF16),
            pltpu.VMEM((6, seq, cols, HALF), BF16),
            pltpu.VMEM((BLK, tokens), F32),
            pltpu.VMEM((HC, tokens, tokens), F32),
            pltpu.VMEM((tokens, tokens), BF16),
            pltpu.VMEM((tokens, tokens), BF16),
            small((2, seq // 8, 2, 2, 2, share, width), BF16),
            small((2, seq // 8, 2, 2, share, width), BF16),
            small((2,) + group, BF16),
            small((2,) + group, BF16),
            small((2,) + group, F32),
            small(group, BF16),
            small(group, BF16),
            small((2, share, width), BF16),
            small((2, share, width), BF16),
            small((2, share, width), F32),
            small((share, width), BF16),
            small((share, width), BF16),
            sems((6,)), sems((6,)),
            sems((5, CHUNKS)), sems((5, CHUNKS)),
            sems((2, CHUNKS)), sems((2, CHUNKS)),
            sems((2, CHUNKS)), sems((2, CHUNKS)),
            sems((CHUNKS,)), sems((CHUNKS,)),
            sems((2, CHUNKS)), sems((2, CHUNKS)),
        ],
        compiler_params=pltpu.CompilerParams(
            collective_id=0, has_side_effects=True, vmem_limit_bytes=58 * 2 ** 20
        ),
        cost_estimate=pl.CostEstimate(
            flops=12 * 10 ** 9, bytes_accessed=11 * 2 ** 20, transcendentals=2 * 2 ** 20
        ),
    )(
        queries.reshape(tokens, feats), keys.reshape(tokens, feats), values.reshape(tokens, feats),
        w_in, out_grad.reshape(tokens, width), block_pattern, col_offset,
    )
    outs = [outs[0]] + [out.reshape(tokens, feats) for out in outs[1:4]] + [outs[4]]
    blocks = [pl.BlockSpec((out.shape[0] // 4, out.shape[1]), lambda n: (n, 0)) for out in outs]
    outs = pl.pallas_call(
        deliver,
        grid=(4,),
        out_shape=[jax.ShapeDtypeStruct(out.shape, out.dtype) for out in outs],
        in_specs=blocks,
        out_specs=blocks,
        compiler_params=pltpu.CompilerParams(vmem_limit_bytes=60 * 2 ** 20),
        cost_estimate=pl.CostEstimate(
            flops=0, bytes_accessed=11 * 2 ** 20, transcendentals=0
        ),
    )(*outs)
    layer_out, q_grad, k_grad, v_grad, w_grad = outs
    if not inside:
        w_grad = lax.psum_scatter(w_grad, ("dp", "seq"), scatter_dimension=0, tiled=True)
        w_grad = w_grad * (dp_count * seq * tokens) ** (-0.5)
    shape = (1, 1, tokens, feats)
    return (
        layer_out.reshape(1, 1, tokens, width),
        q_grad.reshape(shape), k_grad.reshape(shape), v_grad.reshape(shape), w_grad,
    )


def solution(mesh):
    rows = P("dp", "seq", None, None)
    flat = P(("dp", "seq"), None)
    in_specs = (rows, rows, rows, flat, rows, P(), P())
    out_specs = (rows, rows, rows, rows, flat)
    return jax.shard_map(
        functools.partial(shards, mesh.shape["dp"], mesh.shape["seq"]),
        mesh=mesh, in_specs=in_specs, out_specs=out_specs, check_vma=False,
    )
```
